128 devices in a mesh: rows: 32 (over z, y, core), cols: 4 (over x).
Axes of the slice: x: 4, y: 4, z: 4, core: 2. Of those that a mesh axis runs over, the one named last changes fastest.
Arguments:
- basis: float32 [64, 262144], P('cols', 'rows'), may hold values from -450 to 450
- blocks: bfloat16 [1024, 4, 256, 256], P('rows'), may hold values from -16 to 1, as said below
- far_cols: int32 [1024], P('rows'), may hold values from 0 to 1023, as said below
Outputs:
- basis_out: float32 [64, 262144], P('cols', 'rows')
- ritz: float32 [64, 64], P(None, 'cols')
The draws below stay inside these ranges and needn't reach their ends.
Inputs may be any that keep to these rules, and one draw needn't show every extreme that they name: Off-diagonal entries are positive; each diagonal entry of a diagonal block is minus the sum of the other entries of its row over the four blocks, rounded to bfloat16. `far_cols`: the block rows of one device name at most 2 far columns among the block rows of any one device; the block rows of some device are named by exactly 2 block rows of every device.
All inputs are finite; a program needn't handle non-finite values.
Results may differ from the reference program's by a relative error of at most 0.0036.
Values may be sent and summed in bfloat16 or wider, within the bound.
No kernel may reach another device: no remote copies, remote signals or barrier semaphores. Data moves between devices by JAX's collectives and lax.ppermute only.
A program may use at most 128 MiB of HBM per device.

```python
import jax
import jax.numpy as jnp
from jax import lax

BS = 256
MODES = 64
BR_DEV = 32
CAP = 2
ITERS = 4
NB = 1024
NSTATES = 262144


def draw_far_cols(key, part):
    base = jax.random.fold_in(key, 11)
    devices = NB // BR_DEV
    hottest = jax.random.randint(jax.random.fold_in(base, 1), (), 0, devices).astype(jnp.int32)
    pool = (hottest + 1 + jnp.arange((devices - 1) * CAP, dtype=jnp.int32) // CAP) % devices
    device_keys = jax.random.split(jax.random.fold_in(base, 2), devices)

    def per_device(device_key):
        first_key, second_key = jax.random.split(device_key)
        picked = jax.random.permutation(first_key, pool)[:BR_DEV - CAP]
        wanted = jnp.concatenate([jnp.full((CAP,), hottest, jnp.int32), picked.astype(jnp.int32)])
        return jax.random.permutation(second_key, wanted)
    owners = jax.vmap(per_device)(device_keys).astype(jnp.int32)
    local_rows = jax.random.randint(jax.random.fold_in(base, 3), (devices, BR_DEV), 0, BR_DEV).astype(jnp.int32)
    return (owners * BR_DEV + local_rows).reshape(NB).astype(jnp.int32)


def draw_blocks(key, part):
    shape_full = (NB, 4, BS, BS)
    first = jax.random.randint(jax.random.fold_in(key, 1), shape_full, 1, 17)
    second = jax.random.randint(jax.random.fold_in(key, 2), shape_full, 1, 16)
    level = jax.random.randint(jax.random.fold_in(key, 3), (NB, 4, BS, 1), 0, 3)
    factor = jnp.where(level == 2, 4, level + 1).astype(jnp.int32)
    entries = (first * second * factor).astype(jnp.int32)
    strong = (jax.random.randint(jax.random.fold_in(key, 4), (NB, 4, BS, 1), 12, 40) * BS).astype(jnp.int32)
    states = jnp.arange(BS)
    same_state = (states[:, None] == states[None, :])[None, None]
    positions = jnp.arange(4)
    on_diagonal = jnp.logical_and(same_state, (positions == 0)[None, :, None, None])
    on_link = jnp.logical_and(same_state, (positions >= 1)[None, :, None, None])
    linked = jnp.where(on_link, entries + strong, entries).astype(jnp.int32)
    off_entries = jnp.where(on_diagonal, 0, linked).astype(jnp.int32)
    row_total = jnp.sum(jnp.sum(off_entries, axis=3, keepdims=True), axis=1, keepdims=True).astype(jnp.int32)
    scale_factor = 1.0 / (256.0 * BS)
    valued = jnp.where(on_diagonal, -row_total.astype(jnp.float32), off_entries.astype(jnp.float32))
    return (valued * scale_factor).astype(jnp.bfloat16)


def draw_basis(key, part):
    position = jnp.arange(NSTATES, dtype=jnp.float32) / NSTATES
    block_value = jax.random.truncated_normal(jax.random.fold_in(key, 1), -4.0, 4.0, (MODES, NB), jnp.float32)
    noise = jax.random.truncated_normal(jax.random.fold_in(key, 2), -4.0, 4.0, (MODES, NSTATES), jnp.float32)
    common_block = jax.random.truncated_normal(jax.random.fold_in(key, 6), -4.0, 4.0, (NB,), jnp.float32)
    common_noise = jax.random.truncated_normal(jax.random.fold_in(key, 7), -4.0, 4.0, (NSTATES,), jnp.float32)
    common_weight = 0.8
    ramp = 1.0 + 2.0 * position
    mixing = jax.random.uniform(jax.random.fold_in(key, 3), (MODES, 1), jnp.float32, -1.0, 1.0)
    state_scale = jnp.exp(jax.random.uniform(jax.random.fold_in(key, 4), (NSTATES,), jnp.float32, -1.15, 1.15))
    col_scale = jnp.exp(jax.random.uniform(jax.random.fold_in(key, 5), (MODES, 1), jnp.float32, -1.15, 1.15))
    spread_value = jnp.broadcast_to(block_value[:, :, None], (MODES, NB, BS)).reshape(MODES, NSTATES)
    common = jnp.broadcast_to(common_block[:, None], (NB, BS)).reshape(NSTATES) + common_noise
    inner = spread_value + noise + common_weight * mixing * common[None, :]
    return col_scale * state_scale[None, :] * ramp[None, :] * inner


def setup_inputs(seed: int = 0) -> dict:
    arg_keys = jax.random.split(jax.random.key(seed), 4)
    return {
        "basis": draw_basis(jax.random.fold_in(arg_keys[3], 71), 0),
        "blocks": draw_blocks(jax.random.fold_in(arg_keys[3], 71), 0),
        "far_cols": draw_far_cols(jax.random.fold_in(arg_keys[3], 71), 0),
    }


def apply_generator(iterate_bf, blocks, far_cols):
    shaped = iterate_bf.astype(jnp.float32).reshape(MODES, NB, BS)
    pieces = [shaped, jnp.roll(shaped, 1, axis=1), jnp.roll(shaped, -1, axis=1), jnp.take(shaped, far_cols, axis=1)]
    total = jnp.zeros((MODES, NB, BS), jnp.float32)
    for position in range(4):
        total = total + jnp.einsum('jbt,bst->jbs', pieces[position], blocks[:, position].astype(jnp.float32))
    return total.reshape(MODES, NSTATES)

def reference(basis, blocks, far_cols):
    iterate = basis
    for step in range(ITERS):
        iterate = iterate + 0.2 * apply_generator(iterate.astype(jnp.bfloat16), blocks, far_cols)
    applied = apply_generator(iterate.astype(jnp.bfloat16), blocks, far_cols)
    highest = lax.Precision.HIGHEST
    gram = jnp.dot(iterate, iterate.T, precision=highest) / NSTATES
    product = jnp.dot(iterate, applied.T, precision=highest) / NSTATES
    factor = jnp.linalg.cholesky(gram)
    identity_square = jnp.eye(MODES, dtype=factor.dtype)
    inverse_factor = lax.linalg.triangular_solve(factor, identity_square, left_side=True, lower=True)
    basis_out = jnp.dot(inverse_factor, iterate, precision=highest)
    left_part = jnp.dot(inverse_factor, product, precision=highest)
    ritz = jnp.dot(left_part, inverse_factor.T, precision=highest)
    return (basis_out, ritz)
```

```python
import functools

import jax
import jax.numpy as jnp
from jax import lax
from jax.experimental import pallas as pl
from jax.experimental.pallas import tpu as pltpu
from jax.sharding import PartitionSpec as P

ITERS = 4
CAP = 2
STEP = 0.2
NT = (((1,), (1,)), ((), ()))
NN = (((1,), (0,)), ((), ()))
BF = jnp.bfloat16
F32 = jnp.float32
VMEM = pl.BlockSpec(memory_space=pltpu.VMEM)
SMEM = pl.BlockSpec(memory_space=pltpu.SMEM)


def dot(a, b, dims):
    return lax.dot_general(a, b, dims, preferred_element_type=F32)


def exchange(x, axes):
    return lax.all_to_all(x, axes, split_axis=0, concat_axis=0, tiled=True)


def local_kernel(group, rows, size, base, x_ref, w_ref, d_ref, p_ref, n_ref, o_ref):
    step = pl.program_id(0)
    steps = rows // group

    def block(index):
        return x_ref[:, pl.ds(pl.multiple_of(index * size, size), size)]

    for r in range(group):
        b = step * group + r
        low = block(jnp.maximum(b - 1, 0))
        if r == 0:
            low = jnp.where(step > 0, low, jnp.zeros_like(low))
        high = block(jnp.minimum(b + 1, rows - 1))
        if r == group - 1:
            high = jnp.where(step < steps - 1, high, jnp.zeros_like(high))
        acc = dot(block(b), d_ref[r, 0], NT)
        acc += dot(low, p_ref[r, 0], NT)
        acc += dot(high, n_ref[r, 0], NT)
        at = pl.ds(r * size, size)
        o_ref[:, at] = w_ref[:, at] + STEP * acc if base else acc


def local_part(x, w, blocks, base):
    width, states = x.shape
    rows, _, size, _ = blocks.shape
    group = 8
    spec = [pl.BlockSpec((group, 1, size, size), lambda i, k=k: (i, k, 0, 0)) for k in range(3)]
    strip = pl.BlockSpec((width, group * size), lambda i: (0, i))
    return pl.pallas_call(
        functools.partial(local_kernel, group, rows, size, base),
        grid=(rows // group,),
        out_shape=jax.ShapeDtypeStruct((width, states), F32),
        in_specs=[pl.BlockSpec((width, states), lambda i: (0, 0)), strip, *spec],
        out_specs=strip,
        compiler_params=pltpu.CompilerParams(vmem_limit_bytes=16 << 20),
        cost_estimate=pl.CostEstimate(
            flops=6 * width * rows * size * size, bytes_accessed=6 * rows * size * size, transcendentals=0
        ),
    )(x, w, blocks, blocks, blocks)


def far_sum(b, rows, loc_ref, recv_ref, low_ref, high_ref, far_ref):
    acc = dot(recv_ref[loc_ref[b]], far_ref[b], NT)
    if b == 0:
        acc += dot(low_ref[...], far_ref[rows], NT)
    if b == rows - 1:
        acc += dot(high_ref[...], far_ref[rows + 1], NT)
    return acc


def pack(want_ref, x_ref, send_ref, size):
    for s in range(send_ref.shape[0]):
        at = pl.multiple_of(want_ref[s] * size, size)
        send_ref[s] = x_ref[:, pl.ds(at, size)]


def far_kernel(rows, size, copies, want_ref, loc_ref, t_ref, recv_ref, low_ref, high_ref, far_ref,
               w_ref, x_ref, send_ref, first_ref, last_ref, *all_ref):
    for b in range(rows):
        acc = far_sum(b, rows, loc_ref, recv_ref, low_ref, high_ref, far_ref)
        at = pl.ds(b * size, size)
        new = t_ref[:, at] + STEP * acc
        w_ref[:, at] = new
        rounded = new.astype(BF)
        x_ref[:, at] = rounded
        for c in range(copies):
            all_ref[0][c, :, at] = rounded
    first_ref[...] = x_ref[:, :size]
    last_ref[...] = x_ref[:, (rows - 1) * size:]
    pack(want_ref, x_ref, send_ref, size)


def far_part(want, loc, t, recv, low, high, far, copies):
    width, states = t.shape
    size = far.shape[1]
    rows = states // size
    shapes = [
        jax.ShapeDtypeStruct((width, states), F32),
        jax.ShapeDtypeStruct((width, states), BF),
        jax.ShapeDtypeStruct(recv.shape, BF),
        jax.ShapeDtypeStruct((width, size), BF),
        jax.ShapeDtypeStruct((width, size), BF),
    ]
    if copies:
        shapes.append(jax.ShapeDtypeStruct((copies, width, states), BF))
    return pl.pallas_call(
        functools.partial(far_kernel, rows, size, copies),
        out_shape=shapes,
        in_specs=[SMEM, SMEM] + [VMEM] * 5,
        out_specs=[VMEM] * len(shapes),
        compiler_params=pltpu.CompilerParams(vmem_limit_bytes=24 << 20),
        cost_estimate=pl.CostEstimate(
            flops=2 * width * rows * size * size, bytes_accessed=2 * rows * size * size, transcendentals=0
        ),
    )(want, loc, t, recv, low, high, far)


def pack_kernel(size, want_ref, x_ref, send_ref):
    pack(want_ref, x_ref, send_ref, size)


def product_kernel(rows, size, copies, loc_ref, t_ref, recv_ref, low_ref, high_ref, far_ref, all_ref, o_ref, z_ref):
    width = t_ref.shape[0]
    modes = all_ref.shape[0] * width
    for b in range(rows):
        acc = far_sum(b, rows, loc_ref, recv_ref, low_ref, high_ref, far_ref)
        at = pl.ds(b * size, size)
        z = t_ref[:, at] + acc
        top = z.astype(BF)
        z_ref[:width, at] = top
        z_ref[width:, at] = (z - top.astype(F32)).astype(BF)
    total = jnp.zeros((2 * width, modes), F32)
    wide = 2048
    for b in range(rows * size // wide):
        at = pl.ds(b * wide, wide)
        total += dot(z_ref[:, at], all_ref[:, :, at].reshape(modes, wide), NT)
    part = total[:width] + total[width:]
    for c in range(copies):
        o_ref[c] = part


def product_part(loc, t, recv, low, high, far, everyone, copies):
    width, states = t.shape
    size = far.shape[1]
    modes = everyone.shape[0] * width
    rows = states // size
    return pl.pallas_call(
        functools.partial(product_kernel, rows, size, copies),
        out_shape=jax.ShapeDtypeStruct((copies, width, modes), F32),
        in_specs=[SMEM] + [VMEM] * 6,
        out_specs=VMEM,
        scratch_shapes=[pltpu.VMEM((2 * width, states), BF)],
        compiler_params=pltpu.CompilerParams(vmem_limit_bytes=24 << 20),
        cost_estimate=pl.CostEstimate(
            flops=2 * width * rows * size * size, bytes_accessed=2 * rows * size * size, transcendentals=0
        ),
    )(loc, t, recv, low, high, far, everyone)


def gram_kernel(copies, all_ref, o_ref):
    groups, width, states = all_ref.shape
    modes = groups * width
    total = jnp.zeros((modes, modes), F32)
    wide = 2048
    for b in range(states // wide):
        w = all_ref[:, :, pl.ds(b * wide, wide)].reshape(modes, wide)
        total += dot(w, w, NT)
    half = modes // 2
    folded = jnp.concatenate([total[:half], total[half:]], axis=1)
    for c in range(copies):
        o_ref[c] = folded


def gram_part(everyone, copies):
    modes = everyone.shape[0] * everyone.shape[1]
    return pl.pallas_call(
        functools.partial(gram_kernel, copies),
        out_shape=jax.ShapeDtypeStruct((copies, modes // 2, 2 * modes), F32),
        in_specs=[VMEM],
        out_specs=VMEM,
        compiler_params=pltpu.CompilerParams(vmem_limit_bytes=16 << 20),
        cost_estimate=pl.CostEstimate(
            flops=2 * modes * modes * everyone.shape[2], bytes_accessed=2 * everyone.size, transcendentals=0
        ),
    )(everyone)


def inverse_factor(gram):
    n = gram.shape[0]
    row_id = lax.broadcasted_iota(jnp.int32, (n, 2 * n), 0)
    lane = lax.broadcasted_iota(jnp.int32, (n, 2 * n), 1)
    unit = jnp.where(lane == row_id + n, 1.0, 0.0)
    work = jnp.concatenate([gram, unit[:, n:]], axis=1)
    column_id = lax.broadcasted_iota(jnp.int32, (n, 1), 0)
    roots = jnp.zeros((n, 1), F32)
    for j in range(n):
        row = work[j:j + 1]
        pivot = row[:, j:j + 1]
        column = work[:, j:j + 1]
        roots = jnp.where(column_id == j, pivot, roots)
        factor = jnp.where(column_id > j, column / pivot, 0.0)
        work = work - factor * row
    return work[:, n:] * lax.rsqrt(roots)


def finish_kernel(scale, own_ref, parts_ref, all_ref, w_ref, out_ref, inv_ref):
    groups, width, states = all_ref.shape
    modes = groups * width
    total = jnp.sum(parts_ref[...], axis=0) * scale
    gram = jnp.concatenate([total[:, :modes], total[:, modes:]], axis=0)
    inverse = inverse_factor(gram)
    inv_ref[...] = inverse
    start = pl.multiple_of(own_ref[0] * width, width)
    mine = inv_ref[pl.ds(start, width)]
    place = lax.broadcasted_iota(jnp.int32, (modes, width), 0) - lax.broadcasted_iota(jnp.int32, (modes, width), 1)
    pick = jnp.where(place == start, 1.0, 0.0)
    within = lax.dot_general(mine, pick, NN, precision=lax.Precision.HIGHEST, preferred_element_type=F32)
    top = mine.astype(BF)
    rest = (mine - top.astype(F32)).astype(BF)
    left = jnp.concatenate([top, rest], axis=1)
    small = within.astype(BF)
    wide = 1024
    for b in range(states // wide):
        at = pl.ds(b * wide, wide)
        w = all_ref[:, :, at].reshape(modes, wide)
        own = w_ref[:, at]
        low = (own - own.astype(BF).astype(F32)).astype(BF)
        acc = dot(left, jnp.concatenate([w, w], axis=0), NN)
        out_ref[:, at] = acc + dot(small, low, NN)


def finish(own, parts, everyone, w, scale):
    width, states = w.shape
    modes = everyone.shape[0] * width
    return pl.pallas_call(
        functools.partial(finish_kernel, scale),
        out_shape=[jax.ShapeDtypeStruct((width, states), F32), jax.ShapeDtypeStruct((modes, modes), F32)],
        in_specs=[SMEM] + [VMEM] * 3,
        out_specs=[VMEM] * 2,
        compiler_params=pltpu.CompilerParams(vmem_limit_bytes=24 << 20),
        cost_estimate=pl.CostEstimate(flops=1 << 30, bytes_accessed=16 << 20, transcendentals=0),
    )(own, parts, everyone, w)


def ritz_kernel(groups, scale, parts_ref, inv_ref, mine_ref, o_ref):
    copies, width, modes = parts_ref.shape
    parts = parts_ref[...].reshape(copies // groups, modes, modes)
    turned = jnp.sum(parts, axis=0) * scale
    highest = lax.Precision.HIGHEST
    inverse = inv_ref[...]
    half = lax.dot_general(inverse, turned, NT, precision=highest, preferred_element_type=F32)
    o_ref[...] = lax.dot_general(half, mine_ref[...], NT, precision=highest, preferred_element_type=F32)


def body(basis, blocks, far_cols):
    width, states = basis.shape
    rows, _, size, _ = blocks.shape
    devices = lax.axis_size("rows")
    groups = lax.axis_size("cols")
    scale = 1.0 / (states * devices)
    both = ("rows", "cols")

    owner = far_cols // rows
    inside = far_cols % rows
    match = owner[None, :] == jnp.arange(devices, dtype=jnp.int32)[:, None]
    first = jnp.min(jnp.where(match, inside[None, :], rows - 1), axis=1)
    second = jnp.max(jnp.where(match, inside[None, :], 0), axis=1)
    lane = jnp.arange(128, dtype=jnp.int32)[None, None, :]
    asked = jnp.where(lane == 0, first[:, None, None], second[:, None, None])
    answer = exchange(asked, "rows")
    want = jnp.clip(answer[:, 0, :CAP].reshape(devices * CAP), 0, rows - 1)
    earlier = jnp.logical_and(owner[None, :] == owner[:, None], inside[None, :] < inside[:, None])
    loc = owner * CAP + jnp.any(earlier, axis=1).astype(jnp.int32)
    loc = jnp.clip(loc, 0, devices * CAP - 1)

    far = jnp.concatenate([blocks[:, 3], blocks[:1, 1], blocks[-1:, 2]], axis=0)
    up = [(i, (i + 1) % devices) for i in range(devices)]
    down = [(target, source) for source, target in up]

    w = basis
    x = w.astype(BF)
    send = pl.pallas_call(
        functools.partial(pack_kernel, size),
        out_shape=jax.ShapeDtypeStruct((devices * CAP, width, size), BF),
        in_specs=[SMEM, VMEM],
        out_specs=VMEM,
    )(want, x)
    edge_first, edge_last = x[:, :size], x[:, states - size:]
    everyone = None
    for step in range(ITERS):
        recv = exchange(send, "rows")
        low = lax.ppermute(edge_last, "rows", up)
        high = lax.ppermute(edge_first, "rows", down)
        t = local_part(x, w, blocks, True)
        made = far_part(want, loc, t, recv, low, high, far, groups if step == ITERS - 1 else 0)
        w, x, send, edge_first, edge_last = made[:5]
        if step == ITERS - 1:
            everyone = exchange(made[5], "cols")
    recv = exchange(send, "rows")
    low = lax.ppermute(edge_last, "rows", up)
    high = lax.ppermute(edge_first, "rows", down)
    t = local_part(x, w, blocks, False)
    gram_parts = exchange(gram_part(everyone, devices), "rows")
    parts = product_part(loc, t, recv, low, high, far, everyone, devices * groups)
    parts = exchange(parts, both)
    own = lax.axis_index("cols")
    basis_out, inverse = finish(own.reshape(1), gram_parts, everyone, w, scale)
    mine = lax.dynamic_slice_in_dim(inverse, own * width, width, 0)
    modes = groups * width
    ritz = pl.pallas_call(
        functools.partial(ritz_kernel, groups, scale),
        out_shape=jax.ShapeDtypeStruct((modes, width), F32),
        in_specs=[VMEM] * 3,
        out_specs=VMEM,
    )(parts, inverse, mine)
    return (basis_out, ritz)


def solution(mesh):
    in_specs = (P("cols", "rows"), P("rows", None, None, None), P("rows"))
    out_specs = (P("cols", "rows"), P(None, "cols"))
    return jax.shard_map(body, mesh=mesh, in_specs=in_specs, out_specs=out_specs, check_vma=False)
```

```python
import functools

import jax
import jax.numpy as jnp
from jax import lax
from jax.experimental import pallas as pl
from jax.experimental.pallas import tpu as pltpu
from jax.sharding import PartitionSpec as P

ITERS = 4
CAP = 2
GROUPS = 4
AHEAD = 8
LATER = 2
STEP = 0.2
NT = (((1,), (1,)), ((), ()))
NN = (((1,), (0,)), ((), ()))
BF = jnp.bfloat16
F32 = jnp.float32
VMEM = pl.BlockSpec(memory_space=pltpu.VMEM)
SMEM = pl.BlockSpec(memory_space=pltpu.SMEM)
HBM = pl.BlockSpec(memory_space=pltpu.HBM)


def dot(a, b, dims):
    return lax.dot_general(a, b, dims, preferred_element_type=F32)


def exchange(x, axes):
    return lax.all_to_all(x, axes, split_axis=0, concat_axis=0, tiled=True)


def fetch(blocks_ref, first, held_ref, sems):
    rows, count = held_ref.shape[:2]
    group = rows // GROUPS
    copies = []
    for g in range(GROUPS):
        at = pl.ds(g * group, group)
        copies.append(pltpu.make_async_copy(blocks_ref.at[at, pl.ds(first, count)], held_ref.at[at], sems.at[g]))
    for copy in copies:
        copy.start()
    return copies


def local_kernel(rows, size, last, x_ref, *refs):
    if last:
        blocks_ref, o_ref, held_ref, sems = refs
    else:
        w_ref, blocks_ref, o_ref, far_ref, edge_ref, held_ref, sems, far_sems, edge_sems = refs
    copies = fetch(blocks_ref, 0, held_ref, sems)
    if not last:
        later = copy_edges(blocks_ref, edge_ref, edge_sems)
        later.append(pltpu.make_async_copy(blocks_ref.at[pl.ds(0, AHEAD), 3], far_ref, far_sems))
        later[-1].start()
    for b in range(rows):
        if b % (rows // GROUPS) == 0:
            copies[b // (rows // GROUPS)].wait()
        acc = dot(x_ref[:, b * size:(b + 1) * size], held_ref[b, 0], NT)
        if b > 0:
            acc += dot(x_ref[:, (b - 1) * size:b * size], held_ref[b, 1], NT)
        if b < rows - 1:
            acc += dot(x_ref[:, (b + 1) * size:(b + 2) * size], held_ref[b, 2], NT)
        at = pl.ds(b * size, size)
        o_ref[:, at] = acc if last else w_ref[:, at] + STEP * acc
    if not last:
        for copy in later:
            copy.wait()


def local_part(blocks, x, *w):
    width, states = x.shape
    rows, _, size, _ = blocks.shape
    out = [jax.ShapeDtypeStruct((width, states), F32)]
    scratch = [pltpu.VMEM((rows, 3, size, size), BF), pltpu.SemaphoreType.DMA((GROUPS,))]
    if w:
        out += [pltpu.VMEM((AHEAD, size, size), BF), pltpu.VMEM((2, size, size), BF)]
        scratch += [pltpu.SemaphoreType.DMA, pltpu.SemaphoreType.DMA((2,))]
    return pl.pallas_call(
        functools.partial(local_kernel, rows, size, not w),
        out_shape=out,
        in_specs=[VMEM] * (1 + len(w)) + [HBM],
        out_specs=[VMEM] * len(out),
        scratch_shapes=scratch,
        compiler_params=pltpu.CompilerParams(vmem_limit_bytes=24 << 20),
        cost_estimate=pl.CostEstimate(
            flops=6 * width * rows * size * size, bytes_accessed=6 * rows * size * size, transcendentals=0
        ),
    )(x, *w, blocks)


def copy_edges(blocks_ref, edge_ref, sems):
    rows = blocks_ref.shape[0]
    copies = [
        pltpu.make_async_copy(blocks_ref.at[0, 1], edge_ref.at[0], sems.at[0]),
        pltpu.make_async_copy(blocks_ref.at[rows - 1, 2], edge_ref.at[1], sems.at[1]),
    ]
    for copy in copies:
        copy.start()
    return copies


def stream_far(blocks_ref, held_ref, sems):
    ahead = blocks_ref.shape[0] - held_ref.shape[0]
    group = held_ref.shape[0] // LATER
    copies = []
    for g in range(LATER):
        source = blocks_ref.at[pl.ds(ahead + g * group, group), 3]
        copies.append(pltpu.make_async_copy(source, held_ref.at[pl.ds(g * group, group)], sems.at[g]))
    for copy in copies:
        copy.start()

    def wait(b):
        if b >= ahead and (b - ahead) % group == 0:
            copies[(b - ahead) // group].wait()
    return wait


def far_sum(b, rows, loc_ref, recv_ref, low_ref, high_ref, edge_ref, block):
    acc = dot(recv_ref[loc_ref[b]], block, NT)
    if b == 0:
        acc += dot(low_ref[...], edge_ref[0], NT)
    if b == rows - 1:
        acc += dot(high_ref[...], edge_ref[1], NT)
    return acc


def pack(want_ref, x_ref, send_ref, size):
    for s in range(send_ref.shape[0]):
        at = pl.multiple_of(want_ref[s] * size, size)
        send_ref[s] = x_ref[:, pl.ds(at, size)]


def far_kernel(rows, size, want_ref, loc_ref, t_ref, recv_ref, low_ref, high_ref, far_ref, edge_ref,
               blocks_ref, w_ref, x_ref, send_ref, first_ref, last_ref, held_ref, sems):
    wait = stream_far(blocks_ref, held_ref, sems)
    for b in range(rows):
        wait(b)
        block = far_ref[b] if b < AHEAD else held_ref[b - AHEAD]
        acc = far_sum(b, rows, loc_ref, recv_ref, low_ref, high_ref, edge_ref, block)
        at = pl.ds(b * size, size)
        new = t_ref[:, at] + STEP * acc
        w_ref[:, at] = new
        rounded = new.astype(BF)
        x_ref[:, at] = rounded
    first_ref[...] = x_ref[:, :size]
    last_ref[...] = x_ref[:, (rows - 1) * size:]
    pack(want_ref, x_ref, send_ref, size)


def far_part(want, loc, t, recv, low, high, far, edge, blocks):
    width, states = t.shape
    size = far.shape[2]
    rows = states // size
    shapes = [
        jax.ShapeDtypeStruct((width, states), F32),
        jax.ShapeDtypeStruct((width, states), BF),
        jax.ShapeDtypeStruct(recv.shape, BF),
        jax.ShapeDtypeStruct((width, size), BF),
        jax.ShapeDtypeStruct((width, size), BF),
    ]
    return pl.pallas_call(
        functools.partial(far_kernel, rows, size),
        out_shape=shapes,
        in_specs=[SMEM, SMEM] + [VMEM] * 6 + [HBM],
        out_specs=[VMEM] * len(shapes),
        scratch_shapes=[pltpu.VMEM((rows - AHEAD, size, size), BF), pltpu.SemaphoreType.DMA((LATER,))],
        compiler_params=pltpu.CompilerParams(vmem_limit_bytes=16 << 20),
        cost_estimate=pl.CostEstimate(
            flops=2 * width * rows * size * size, bytes_accessed=2 * rows * size * size, transcendentals=0
        ),
    )(want, loc, t, recv, low, high, far, edge, blocks)


def product_kernel(rows, size, copies, loc_ref, t_ref, recv_ref, low_ref, high_ref, blocks_ref,
                   all_ref, o_ref, z_ref, held_ref, edge_ref, sems, edge_sems):
    width = t_ref.shape[0]
    modes = all_ref.shape[0] * width
    edges = copy_edges(blocks_ref, edge_ref, edge_sems)
    wait = stream_far(blocks_ref, held_ref, sems)
    for edge in edges:
        edge.wait()
    for b in range(rows):
        wait(b)
        acc = far_sum(b, rows, loc_ref, recv_ref, low_ref, high_ref, edge_ref, held_ref[b])
        at = pl.ds(b * size, size)
        z = t_ref[:, at] + acc
        top = z.astype(BF)
        z_ref[:width, at] = top
        z_ref[width:, at] = (z - top.astype(F32)).astype(BF)
    total = jnp.zeros((2 * width, modes), F32)
    for start, w in strips(all_ref):
        total += dot(z_ref[:, start:start + w.shape[1]], w, NT)
    part = total[:width] + total[width:]
    folded = jnp.concatenate([part[:width // 2], part[width // 2:]], axis=1)
    for c in range(copies):
        o_ref[c] = folded


def strips(all_ref, wide=2048):
    groups, width, states = all_ref.shape
    for start in range(0, states, wide):
        yield start, all_ref[:, :, start:start + wide].reshape(groups * width, wide)


def product_part(loc, t, recv, low, high, blocks, everyone, copies):
    width, states = t.shape
    size = blocks.shape[2]
    modes = everyone.shape[0] * width
    rows = states // size
    return pl.pallas_call(
        functools.partial(product_kernel, rows, size, copies),
        out_shape=jax.ShapeDtypeStruct((copies, width // 2, 2 * modes), F32),
        in_specs=[SMEM] + [VMEM] * 4 + [HBM, VMEM],
        out_specs=VMEM,
        scratch_shapes=[
            pltpu.VMEM((2 * width, states), BF),
            pltpu.VMEM((rows, size, size), BF),
            pltpu.VMEM((2, size, size), BF),
            pltpu.SemaphoreType.DMA((LATER,)),
            pltpu.SemaphoreType.DMA((2,)),
        ],
        compiler_params=pltpu.CompilerParams(vmem_limit_bytes=16 << 20),
        cost_estimate=pl.CostEstimate(
            flops=2 * width * rows * size * size, bytes_accessed=2 * rows * size * size, transcendentals=0
        ),
    )(loc, t, recv, low, high, blocks, everyone)


def gram_kernel(own_ref, *refs):
    pieces, (o_ref, all_ref) = refs[:-2], refs[-2:]
    groups = len(pieces)
    for k, piece in enumerate(pieces):
        all_ref[lax.rem(own_ref[0] + groups - k, groups)] = piece[...]
    modes = groups * all_ref.shape[1]
    total = jnp.zeros((modes, modes), F32)
    for _, w in strips(all_ref):
        total += dot(w, w, NT)
    folded = jnp.concatenate([total[:modes // 2], total[modes // 2:]], axis=1)
    for c in range(o_ref.shape[0]):
        o_ref[c] = folded


def gram_part(own, pieces, copies):
    groups = len(pieces)
    width, states = pieces[0].shape
    modes = groups * width
    return pl.pallas_call(
        gram_kernel,
        out_shape=[
            jax.ShapeDtypeStruct((copies, modes // 2, 2 * modes), F32),
            jax.ShapeDtypeStruct((groups, width, states), BF),
        ],
        in_specs=[SMEM] + [VMEM] * groups,
        out_specs=[VMEM] * 2,
        compiler_params=pltpu.CompilerParams(vmem_limit_bytes=16 << 20),
        cost_estimate=pl.CostEstimate(
            flops=2 * modes * modes * states, bytes_accessed=4 * modes * states, transcendentals=0
        ),
    )(own, *pieces)


def inverse_factor(gram):
    n = gram.shape[0]
    row_id = lax.broadcasted_iota(jnp.int32, (n, 2 * n), 0)
    lane = lax.broadcasted_iota(jnp.int32, (n, 2 * n), 1)
    unit = jnp.where(lane == row_id + n, 1.0, 0.0)
    work = jnp.concatenate([gram, unit[:, n:]], axis=1)
    column_id = lax.broadcasted_iota(jnp.int32, (n, 1), 0)
    roots = jnp.zeros((n, 1), F32)
    for j in range(n):
        row = work[j:j + 1]
        pivot = row[:, j:j + 1]
        column = work[:, j:j + 1]
        roots = jnp.where(column_id == j, pivot, roots)
        factor = jnp.where(column_id > j, column / pivot, 0.0)
        work = work - factor * row
    return work[:, n:] * lax.rsqrt(roots)


def finish_kernel(scale, own_ref, parts_ref, all_ref, w_ref, out_ref, inv_ref):
    groups, width, _ = all_ref.shape
    modes = groups * width
    total = jnp.sum(parts_ref[...], axis=0) * scale
    gram = jnp.concatenate([total[:, :modes], total[:, modes:]], axis=0)
    inv_ref[...] = inverse_factor(gram)
    start = pl.multiple_of(own_ref[0] * width, width)
    mine = inv_ref[pl.ds(start, width)]
    place = lax.broadcasted_iota(jnp.int32, (modes, width), 0) - lax.broadcasted_iota(jnp.int32, (modes, width), 1)
    pick = jnp.where(place == start, 1.0, 0.0)
    within = lax.dot_general(mine, pick, NN, precision=lax.Precision.HIGHEST, preferred_element_type=F32)
    top = mine.astype(BF)
    rest = (mine - top.astype(F32)).astype(BF)
    left = jnp.concatenate([top, rest], axis=1)
    small = within.astype(BF)
    for first, w in strips(all_ref, 1024):
        at = pl.ds(first, w.shape[1])
        own = w_ref[:, at]
        low = (own - own.astype(BF).astype(F32)).astype(BF)
        acc = dot(left, jnp.concatenate([w, w], axis=0), NN)
        out_ref[:, at] = acc + dot(small, low, NN)


def finish(own, parts, everyone, w, scale):
    width, states = w.shape
    modes = everyone.shape[0] * width
    return pl.pallas_call(
        functools.partial(finish_kernel, scale),
        out_shape=[jax.ShapeDtypeStruct((width, states), F32), jax.ShapeDtypeStruct((modes, modes), F32)],
        in_specs=[SMEM] + [VMEM] * 3,
        out_specs=[VMEM] * 2,
        compiler_params=pltpu.CompilerParams(vmem_limit_bytes=16 << 20),
        cost_estimate=pl.CostEstimate(flops=1 << 30, bytes_accessed=16 << 20, transcendentals=0),
    )(own, parts, everyone, w)


def ritz_kernel(groups, scale, own_ref, parts_ref, inv_ref, o_ref):
    copies, half, wide = parts_ref.shape
    modes = wide // 2
    width = 2 * half
    turned = []
    for c in range(groups):
        total = parts_ref[c]
        for r in range(1, copies // groups):
            total = total + parts_ref[r * groups + c]
        turned += [total[:, :modes], total[:, modes:]]
    turned = jnp.concatenate(turned, axis=0) * scale
    highest = lax.Precision.HIGHEST
    start = pl.multiple_of(own_ref[0] * width, width)
    mine = inv_ref[pl.ds(start, width)]
    part = lax.dot_general(mine, turned, NN, precision=highest, preferred_element_type=F32)
    o_ref[...] = lax.dot_general(part, inv_ref[...], NT, precision=highest, preferred_element_type=F32)


def ask_kernel(rows, far_ref, o_ref):
    devices, lanes = o_ref.shape
    far = far_ref[...]
    owner = lax.broadcasted_iota(jnp.int32, (devices, rows), 0)
    inside = jnp.broadcast_to(far, (devices, rows)) - owner * rows
    match = jnp.logical_and(inside >= 0, inside < rows)
    first = jnp.min(jnp.where(match, inside, rows - 1), axis=1, keepdims=True)
    second = jnp.max(jnp.where(match, inside, 0), axis=1, keepdims=True)
    lane = lax.broadcasted_iota(jnp.int32, (devices, lanes), 1)
    o_ref[...] = jnp.where(lane == 0, first, second)


def first_pack_kernel(size, rows, answer_ref, x_ref, send_ref):
    for s in range(send_ref.shape[0]):
        block = jnp.clip(answer_ref[s // CAP, 0, s % CAP], 0, rows - 1)
        at = pl.multiple_of(block * size, size)
        send_ref[s] = x_ref[:, pl.ds(at, size)]


def body(basis, blocks, far_cols):
    width, states = basis.shape
    rows, _, size, _ = blocks.shape
    devices = lax.axis_size("rows")
    groups = lax.axis_size("cols")
    scale = 1.0 / (states * devices)
    both = ("rows", "cols")

    asked = pl.pallas_call(
        functools.partial(ask_kernel, rows),
        out_shape=jax.ShapeDtypeStruct((devices, 128), jnp.int32),
        in_specs=[VMEM],
        out_specs=VMEM,
        compiler_params=pltpu.CompilerParams(vmem_limit_bytes=1 << 20),
    )(far_cols.reshape(1, rows))
    answer = exchange(asked.reshape(devices, 1, 128), "rows")
    want = jnp.clip(answer[:, 0, :CAP].reshape(devices * CAP), 0, rows - 1)
    owner = far_cols // rows
    inside = far_cols % rows
    earlier = jnp.logical_and(owner[None, :] == owner[:, None], inside[None, :] < inside[:, None])
    loc = owner * CAP + jnp.any(earlier, axis=1).astype(jnp.int32)
    loc = jnp.clip(loc, 0, devices * CAP - 1)

    up = [(i, (i + 1) % devices) for i in range(devices)]
    down = [(target, source) for source, target in up]

    blocks = pltpu.with_memory_space_constraint(blocks, pltpu.HBM)
    w = basis
    x = w.astype(BF)
    send = pl.pallas_call(
        functools.partial(first_pack_kernel, size, rows),
        out_shape=jax.ShapeDtypeStruct((devices * CAP, width, size), BF),
        in_specs=[SMEM, VMEM],
        out_specs=VMEM,
        compiler_params=pltpu.CompilerParams(vmem_limit_bytes=2 << 20),
    )(answer, x)
    edge_first, edge_last = x[:, :size], x[:, states - size:]
    for _ in range(ITERS):
        recv = exchange(send, "rows")
        low = lax.ppermute(edge_last, "rows", up)
        high = lax.ppermute(edge_first, "rows", down)
        t, far, edge = local_part(blocks, x, w)
        w, x, send, edge_first, edge_last = far_part(want, loc, t, recv, low, high, far, edge, blocks)
    recv = exchange(send, "rows")
    pieces = [x]
    for k in range(1, groups):
        pieces.append(lax.ppermute(x, "cols", [(i, (i + k) % groups) for i in range(groups)]))
    low = lax.ppermute(edge_last, "rows", up)
    high = lax.ppermute(edge_first, "rows", down)
    t, = local_part(blocks, x)
    own = lax.axis_index("cols").reshape(1)
    pieces, t, low, high = lax.optimization_barrier((pieces, t, low, high))
    grams, everyone = gram_part(own, pieces, devices)
    w, t, everyone = (pltpu.with_memory_space_constraint(a, pltpu.HBM) for a in (w, t, everyone))
    gram_parts = exchange(grams, "rows")
    parts = product_part(loc, t, recv, low, high, blocks, everyone, devices * groups)
    parts = exchange(parts, both)
    basis_out, inverse = finish(own, gram_parts, everyone, w, scale)
    turned = pl.pallas_call(
        functools.partial(ritz_kernel, groups, scale),
        out_shape=jax.ShapeDtypeStruct((width, groups * width), F32),
        in_specs=[SMEM, VMEM, VMEM],
        out_specs=VMEM,
        compiler_params=pltpu.CompilerParams(vmem_limit_bytes=4 << 20),
    )(own, parts, inverse)
    ritz = turned.T
    return (basis_out, ritz)


def solution(mesh):
    in_specs = (P("cols", "rows"), P("rows", None, None, None), P("rows"))
    out_specs = (P("cols", "rows"), P(None, "cols"))
    return jax.shard_map(body, mesh=mesh, in_specs=in_specs, out_specs=out_specs, check_vma=False)
```

```python
import functools

import jax
import jax.numpy as jnp
from jax import lax
from jax.experimental import pallas as pl
from jax.experimental.pallas import tpu as pltpu
from jax.sharding import PartitionSpec as P

ITERS = 4
CAP = 2
GROUPS = 4
AHEAD = 8
LATER = 2
STEP = 0.2
NT = (((1,), (1,)), ((), ()))
NN = (((1,), (0,)), ((), ()))
BF = jnp.bfloat16
F32 = jnp.float32
VMEM = pl.BlockSpec(memory_space=pltpu.VMEM)
SMEM = pl.BlockSpec(memory_space=pltpu.SMEM)
HBM = pl.BlockSpec(memory_space=pltpu.HBM)


def dot(a, b, dims):
    return lax.dot_general(a, b, dims, preferred_element_type=F32)


def exchange(x, axes):
    return lax.all_to_all(x, axes, split_axis=0, concat_axis=0, tiled=True)


def fetch(blocks_ref, first, held_ref, sems):
    rows, count = held_ref.shape[:2]
    group = rows // GROUPS
    copies = []
    for g in range(GROUPS):
        at = pl.ds(g * group, group)
        copies.append(pltpu.make_async_copy(blocks_ref.at[at, pl.ds(first, count)], held_ref.at[at], sems.at[g]))
    for copy in copies:
        copy.start()
    return copies


def local_kernel(rows, size, last, x_ref, *refs):
    if last:
        blocks_ref, o_ref, held_ref, sems = refs
    else:
        w_ref, blocks_ref, o_ref, far_ref, held_ref, sems, far_sem = refs
    copies = fetch(blocks_ref, 0, held_ref, sems)
    if not last:
        later = pltpu.make_async_copy(blocks_ref.at[pl.ds(0, AHEAD), 3], far_ref, far_sem)
        later.start()
    for b in range(rows):
        if b % (rows // GROUPS) == 0:
            copies[b // (rows // GROUPS)].wait()
        acc = dot(x_ref[:, b * size:(b + 1) * size], held_ref[b, 0], NT)
        if b > 0:
            acc += dot(x_ref[:, (b - 1) * size:b * size], held_ref[b, 1], NT)
        if b < rows - 1:
            acc += dot(x_ref[:, (b + 1) * size:(b + 2) * size], held_ref[b, 2], NT)
        at = pl.ds(b * size, size)
        o_ref[:, at] = acc if last else w_ref[:, at] + STEP * acc
    if not last:
        later.wait()


def local_part(blocks, x, *w):
    width, states = x.shape
    rows, _, size, _ = blocks.shape
    out = [jax.ShapeDtypeStruct((width, states), F32)]
    scratch = [pltpu.VMEM((rows, 3, size, size), BF), pltpu.SemaphoreType.DMA((GROUPS,))]
    if w:
        out.append(pltpu.VMEM((AHEAD, size, size), BF))
        scratch.append(pltpu.SemaphoreType.DMA)
    return pl.pallas_call(
        functools.partial(local_kernel, rows, size, not w),
        out_shape=out,
        in_specs=[VMEM] * (1 + len(w)) + [HBM],
        out_specs=[VMEM] * len(out),
        scratch_shapes=scratch,
        compiler_params=pltpu.CompilerParams(vmem_limit_bytes=24 << 20),
        cost_estimate=pl.CostEstimate(
            flops=6 * width * rows * size * size, bytes_accessed=6 * rows * size * size, transcendentals=0
        ),
    )(x, *w, blocks)


def stream_far(blocks_ref, held_ref, edge_ref, sems):
    rows = blocks_ref.shape[0]
    ahead = rows - held_ref.shape[0]
    group = held_ref.shape[0] // LATER
    copies = []
    for g in range(LATER):
        source = blocks_ref.at[pl.ds(ahead + g * group, group), 3]
        copies.append(pltpu.make_async_copy(source, held_ref.at[pl.ds(g * group, group)], sems.at[g]))
    copies.append(pltpu.make_async_copy(blocks_ref.at[0, 1], edge_ref.at[0], sems.at[LATER]))
    copies.append(pltpu.make_async_copy(blocks_ref.at[rows - 1, 2], edge_ref.at[1], sems.at[LATER + 1]))
    for copy in copies:
        copy.start()
    waiting = set(range(LATER + 2))

    def wait(b):
        needed = []
        if b >= ahead:
            needed.append((b - ahead) // group)
        if b in (0, rows - 1):
            needed += [LATER, LATER + 1]
        for k in needed:
            if k in waiting:
                waiting.remove(k)
                copies[k].wait()
    return wait


def stream_scratch(held, size):
    return [
        pltpu.VMEM((held, size, size), BF),
        pltpu.VMEM((2, size, size), BF),
        pltpu.SemaphoreType.DMA((LATER + 2,)),
    ]


def far_sum(b, rows, odd_ref, loc_ref, recv_ref, pair_ref, other_ref, edge_ref, block):
    acc = dot(recv_ref[loc_ref[b]], block, NT)
    odd = odd_ref[0] == 1
    if b == 0:
        acc += dot(jnp.where(odd, pair_ref[...], other_ref[...]), edge_ref[0], NT)
    if b == rows - 1:
        acc += dot(jnp.where(odd, other_ref[...], pair_ref[...]), edge_ref[1], NT)
    return acc


def block_order(rows):
    return [*range(1, rows), 0]


def pack(want_ref, x_ref, send_ref, size):
    for s in range(send_ref.shape[0]):
        at = pl.multiple_of(want_ref[s] * size, size)
        send_ref[s] = x_ref[:, pl.ds(at, size)]


def far_kernel(rows, size, odd_ref, want_ref, loc_ref, t_ref, recv_ref, pair_ref, other_ref, far_ref, blocks_ref,
               w_ref, x_ref, send_ref, to_pair_ref, to_other_ref, held_ref, edge_ref, sems):
    wait = stream_far(blocks_ref, held_ref, edge_ref, sems)
    for b in block_order(rows):
        wait(b)
        block = far_ref[b] if b < AHEAD else held_ref[b - AHEAD]
        acc = far_sum(b, rows, odd_ref, loc_ref, recv_ref, pair_ref, other_ref, edge_ref, block)
        at = pl.ds(b * size, size)
        new = t_ref[:, at] + STEP * acc
        w_ref[:, at] = new
        x_ref[:, at] = new.astype(BF)
    last = (rows - 1) * size
    to_pair_ref[...] = x_ref[:, pl.ds(pl.multiple_of((1 - odd_ref[0]) * last, size), size)]
    to_other_ref[...] = x_ref[:, pl.ds(pl.multiple_of(odd_ref[0] * last, size), size)]
    pack(want_ref, x_ref, send_ref, size)


def far_part(odd, want, loc, t, recv, pair, other, far, blocks):
    width, states = t.shape
    size = far.shape[2]
    rows = states // size
    shapes = [
        jax.ShapeDtypeStruct((width, states), F32),
        jax.ShapeDtypeStruct((width, states), BF),
        jax.ShapeDtypeStruct(recv.shape, BF),
        jax.ShapeDtypeStruct((width, size), BF),
        jax.ShapeDtypeStruct((width, size), BF),
    ]
    return pl.pallas_call(
        functools.partial(far_kernel, rows, size),
        out_shape=shapes,
        in_specs=[SMEM] * 3 + [VMEM] * 5 + [HBM],
        out_specs=[VMEM] * len(shapes),
        scratch_shapes=stream_scratch(rows - AHEAD, size),
        compiler_params=pltpu.CompilerParams(vmem_limit_bytes=16 << 20),
        cost_estimate=pl.CostEstimate(
            flops=2 * width * rows * size * size, bytes_accessed=2 * rows * size * size, transcendentals=0
        ),
    )(odd, want, loc, t, recv, pair, other, far, blocks)


def product_kernel(rows, size, copies, odd_ref, loc_ref, t_ref, recv_ref, pair_ref, other_ref, blocks_ref, all_ref,
                   o_ref, z_ref, held_ref, edge_ref, sems):
    width = t_ref.shape[0]
    modes = all_ref.shape[0] * width
    wait = stream_far(blocks_ref, held_ref, edge_ref, sems)
    for b in block_order(rows):
        wait(b)
        acc = far_sum(b, rows, odd_ref, loc_ref, recv_ref, pair_ref, other_ref, edge_ref, held_ref[b])
        at = pl.ds(b * size, size)
        z = t_ref[:, at] + acc
        top = z.astype(BF)
        z_ref[:width, at] = top
        z_ref[width:, at] = (z - top.astype(F32)).astype(BF)
    total = jnp.zeros((2 * width, modes), F32)
    for start, w in strips(all_ref):
        total += dot(z_ref[:, start:start + w.shape[1]], w, NT)
    part = total[:width] + total[width:]
    folded = jnp.concatenate([part[:width // 2], part[width // 2:]], axis=1)
    for c in range(copies):
        o_ref[c] = folded


def strips(all_ref, wide=2048):
    groups, width, states = all_ref.shape
    for start in range(0, states, wide):
        yield start, all_ref[:, :, start:start + wide].reshape(groups * width, wide)


def product_part(odd, loc, t, recv, pair, other, blocks, everyone, copies):
    width, states = t.shape
    size = blocks.shape[2]
    modes = everyone.shape[0] * width
    rows = states // size
    return pl.pallas_call(
        functools.partial(product_kernel, rows, size, copies),
        out_shape=jax.ShapeDtypeStruct((copies, width // 2, 2 * modes), F32),
        in_specs=[SMEM] * 2 + [VMEM] * 4 + [HBM, VMEM],
        out_specs=VMEM,
        scratch_shapes=[
            pltpu.VMEM((2 * width, states), BF),
            *stream_scratch(rows, size),
        ],
        compiler_params=pltpu.CompilerParams(vmem_limit_bytes=16 << 20),
        cost_estimate=pl.CostEstimate(
            flops=2 * width * rows * size * size, bytes_accessed=2 * rows * size * size, transcendentals=0
        ),
    )(odd, loc, t, recv, pair, other, blocks, everyone)


def gram_kernel(own_ref, *refs):
    pieces, (o_ref, all_ref) = refs[:-2], refs[-2:]
    groups = len(pieces)
    for k, piece in enumerate(pieces):
        all_ref[lax.rem(own_ref[0] + groups - k, groups)] = piece[...]
    modes = groups * all_ref.shape[1]
    total = jnp.zeros((modes, modes), F32)
    for _, w in strips(all_ref):
        total += dot(w, w, NT)
    packed = pack_lower(total)
    for c in range(o_ref.shape[0]):
        o_ref[c] = packed


def pack_lower(a):
    q = a.shape[0] // 4
    full = jnp.concatenate([a[3 * q:], a[2 * q:3 * q, :3 * q], a[:q, :q]], axis=1)
    second = a[q:2 * q, :2 * q]
    rest = jnp.concatenate([second[:q // 2], second[q // 2:], jnp.zeros((q // 2, 4 * q), a.dtype)], axis=1)
    return jnp.concatenate([full, rest], axis=0)


def unpack_lower(p):
    q = p.shape[1] // 8
    full, rest = p[:q], p[q:]
    second = jnp.concatenate([rest[:, :2 * q], rest[:, 2 * q:4 * q]], axis=0)
    strips = [full[:, 7 * q:], second, full[:, 4 * q:7 * q], full[:, :4 * q]]
    padded = [jnp.concatenate([s, jnp.zeros((q, 4 * q - s.shape[1]), p.dtype)], axis=1) for s in strips[:3]]
    lower = jnp.concatenate([*padded, strips[3]], axis=0)
    row = lax.broadcasted_iota(jnp.int32, lower.shape, 0)
    column = lax.broadcasted_iota(jnp.int32, lower.shape, 1)
    return jnp.where(row >= column, lower, lower.T)


def gram_part(own, pieces, copies):
    groups = len(pieces)
    width, states = pieces[0].shape
    modes = groups * width
    return pl.pallas_call(
        gram_kernel,
        out_shape=[
            jax.ShapeDtypeStruct((copies, 3 * modes // 8, 2 * modes), F32),
            jax.ShapeDtypeStruct((groups, width, states), BF),
        ],
        in_specs=[SMEM] + [VMEM] * groups,
        out_specs=[VMEM] * 2,
        compiler_params=pltpu.CompilerParams(vmem_limit_bytes=16 << 20),
        cost_estimate=pl.CostEstimate(
            flops=2 * modes * modes * states, bytes_accessed=4 * modes * states, transcendentals=0
        ),
    )(own, *pieces)


def inverse_factor(gram):
    n = gram.shape[0]
    row_id = lax.broadcasted_iota(jnp.int32, (n, 2 * n), 0)
    lane = lax.broadcasted_iota(jnp.int32, (n, 2 * n), 1)
    unit = jnp.where(lane == row_id + n, 1.0, 0.0)
    work = jnp.concatenate([gram, unit[:, n:]], axis=1)
    column_id = lax.broadcasted_iota(jnp.int32, (n, 1), 0)
    roots = jnp.zeros((n, 1), F32)
    for j in range(n):
        row = work[j:j + 1]
        pivot = row[:, j:j + 1]
        column = work[:, j:j + 1]
        roots = jnp.where(column_id == j, pivot, roots)
        factor = jnp.where(column_id > j, column / pivot, 0.0)
        work = work - factor * row
    return work[:, n:] * lax.rsqrt(roots)


def finish_kernel(scale, own_ref, parts_ref, all_ref, w_ref, out_ref, inv_ref):
    groups, width, _ = all_ref.shape
    modes = groups * width
    total = jnp.sum(parts_ref[...], axis=0) * scale
    inv_ref[...] = inverse_factor(unpack_lower(total))
    start = pl.multiple_of(own_ref[0] * width, width)
    mine = inv_ref[pl.ds(start, width)]
    place = lax.broadcasted_iota(jnp.int32, (modes, width), 0) - lax.broadcasted_iota(jnp.int32, (modes, width), 1)
    pick = jnp.where(place == start, 1.0, 0.0)
    within = lax.dot_general(mine, pick, NN, precision=lax.Precision.HIGHEST, preferred_element_type=F32)
    top = mine.astype(BF)
    rest = (mine - top.astype(F32)).astype(BF)
    left = jnp.concatenate([top, rest], axis=1)
    small = within.astype(BF)
    for first, w in strips(all_ref, 1024):
        at = pl.ds(first, w.shape[1])
        own = w_ref[:, at]
        low = (own - own.astype(BF).astype(F32)).astype(BF)
        acc = dot(left, jnp.concatenate([w, w], axis=0), NN)
        out_ref[:, at] = acc + dot(small, low, NN)


def finish(own, parts, everyone, w, scale):
    width, states = w.shape
    modes = everyone.shape[0] * width
    return pl.pallas_call(
        functools.partial(finish_kernel, scale),
        out_shape=[jax.ShapeDtypeStruct((width, states), F32), jax.ShapeDtypeStruct((modes, modes), F32)],
        in_specs=[SMEM] + [VMEM] * 3,
        out_specs=[VMEM] * 2,
        compiler_params=pltpu.CompilerParams(vmem_limit_bytes=16 << 20),
        cost_estimate=pl.CostEstimate(flops=1 << 30, bytes_accessed=16 << 20, transcendentals=0),
    )(own, parts, everyone, w)


def ritz_kernel(groups, scale, own_ref, parts_ref, inv_ref, o_ref):
    copies, half, wide = parts_ref.shape
    modes = wide // 2
    width = 2 * half
    turned = []
    for c in range(groups):
        total = parts_ref[c]
        for r in range(1, copies // groups):
            total = total + parts_ref[r * groups + c]
        turned += [total[:, :modes], total[:, modes:]]
    turned = jnp.concatenate(turned, axis=0) * scale
    highest = lax.Precision.HIGHEST
    start = pl.multiple_of(own_ref[0] * width, width)
    mine = inv_ref[pl.ds(start, width)]
    part = lax.dot_general(mine, turned, NN, precision=highest, preferred_element_type=F32)
    o_ref[...] = lax.dot_general(part, inv_ref[...], NT, precision=highest, preferred_element_type=F32)


def ask_kernel(rows, far_ref, o_ref):
    devices, lanes = o_ref.shape
    owner = lax.broadcasted_iota(jnp.int32, (devices, rows), 0)
    inside = jnp.broadcast_to(far_ref[...], (devices, rows)) - owner * rows
    match = jnp.logical_and(inside >= 0, inside < rows)
    first = jnp.min(jnp.where(match, inside, rows - 1), axis=1, keepdims=True)
    second = jnp.max(jnp.where(match, inside, 0), axis=1, keepdims=True)
    lane = lax.broadcasted_iota(jnp.int32, (devices, lanes), 1)
    o_ref[...] = jnp.where(lane == 0, first, second)


def first_pack_kernel(size, rows, answer_ref, x_ref, send_ref):
    for s in range(send_ref.shape[0]):
        block = jnp.clip(answer_ref[s // CAP, 0, s % CAP], 0, rows - 1)
        at = pl.multiple_of(block * size, size)
        send_ref[s] = x_ref[:, pl.ds(at, size)]


def body(basis, blocks, far_cols):
    width, states = basis.shape
    rows, _, size, _ = blocks.shape
    devices = lax.axis_size("rows")
    groups = lax.axis_size("cols")
    scale = 1.0 / (states * devices)
    both = ("rows", "cols")

    asked = pl.pallas_call(
        functools.partial(ask_kernel, rows),
        out_shape=jax.ShapeDtypeStruct((devices, 128), jnp.int32),
        in_specs=[VMEM],
        out_specs=VMEM,
        compiler_params=pltpu.CompilerParams(vmem_limit_bytes=1 << 20),
    )(far_cols.reshape(1, rows))
    answer = exchange(asked.reshape(devices, 1, 128), "rows")
    want = jnp.clip(answer[:, 0, :CAP].reshape(devices * CAP), 0, rows - 1)
    owner = far_cols // rows
    inside = far_cols % rows
    earlier = jnp.logical_and(owner[None, :] == owner[:, None], inside[None, :] < inside[:, None])
    loc = owner * CAP + jnp.any(earlier, axis=1).astype(jnp.int32)
    loc = jnp.clip(loc, 0, devices * CAP - 1)

    pairs = [(i, i + 1 - 2 * (i % 2)) for i in range(devices)]
    others = [(i, (i - 1 + 2 * (i % 2)) % devices) for i in range(devices)]
    odd = (lax.axis_index("rows") % 2).astype(jnp.int32)

    blocks = pltpu.with_memory_space_constraint(blocks, pltpu.HBM)
    w = basis
    x = w.astype(BF)
    send = pl.pallas_call(
        functools.partial(first_pack_kernel, size, rows),
        out_shape=jax.ShapeDtypeStruct((devices * CAP, width, size), BF),
        in_specs=[SMEM, VMEM],
        out_specs=VMEM,
        compiler_params=pltpu.CompilerParams(vmem_limit_bytes=2 << 20),
    )(answer, x)
    last = states - size
    to_pair = lax.dynamic_slice_in_dim(x, (1 - odd) * last, size, 1)
    to_other = lax.dynamic_slice_in_dim(x, odd * last, size, 1)
    odd = odd.reshape(1)
    for _ in range(ITERS):
        recv = exchange(send, "rows")
        pair = lax.ppermute(to_pair, "rows", pairs)
        other = lax.ppermute(to_other, "rows", others)
        t, far = local_part(blocks, x, w)
        w, x, send, to_pair, to_other = far_part(odd, want, loc, t, recv, pair, other, far, blocks)
    recv = exchange(send, "rows")
    pieces = [x]
    for k in range(1, groups):
        pieces.append(lax.ppermute(x, "cols", [(i, (i + k) % groups) for i in range(groups)]))
    pair = lax.ppermute(to_pair, "rows", pairs)
    other = lax.ppermute(to_other, "rows", others)
    t, = local_part(blocks, x)
    own = lax.axis_index("cols").reshape(1)
    pieces, t, pair, other = lax.optimization_barrier((pieces, t, pair, other))
    grams, everyone = gram_part(own, pieces, devices)
    gram_parts = exchange(grams, "rows")
    parts = product_part(odd, loc, t, recv, pair, other, blocks, everyone, devices * groups)
    parts = exchange(parts, both)
    basis_out, inverse = finish(own, gram_parts, everyone, w, scale)
    turned = pl.pallas_call(
        functools.partial(ritz_kernel, groups, scale),
        out_shape=jax.ShapeDtypeStruct((width, groups * width), F32),
        in_specs=[SMEM, VMEM, VMEM],
        out_specs=VMEM,
        compiler_params=pltpu.CompilerParams(vmem_limit_bytes=4 << 20),
    )(own, parts, inverse)
    ritz = turned.T
    return (basis_out, ritz)


def solution(mesh):
    in_specs = (P("cols", "rows"), P("rows", None, None, None), P("rows"))
    out_specs = (P("cols", "rows"), P(None, "cols"))
    return jax.shard_map(body, mesh=mesh, in_specs=in_specs, out_specs=out_specs, check_vma=False)
```

```python
import functools

import jax
import jax.numpy as jnp
from jax import lax
from jax.experimental import pallas as pl
from jax.experimental.pallas import tpu as pltpu
from jax.sharding import PartitionSpec as P

ITERS = 4
CAP = 2
GROUPS = 4
AHEAD = 8
LATER = 2
STEP = 0.2
NT = (((1,), (1,)), ((), ()))
NN = (((1,), (0,)), ((), ()))
BF = jnp.bfloat16
F32 = jnp.float32
VMEM = pl.BlockSpec(memory_space=pltpu.VMEM)
SMEM = pl.BlockSpec(memory_space=pltpu.SMEM)
HBM = pl.BlockSpec(memory_space=pltpu.HBM)


def dot(a, b, dims):
    return lax.dot_general(a, b, dims, preferred_element_type=F32)


def exchange(x, axes):
    return lax.all_to_all(x, axes, split_axis=0, concat_axis=0, tiled=True)


def fetch(blocks_ref, first, held_ref, sems):
    rows, count = held_ref.shape[:2]
    group = rows // GROUPS
    copies = []
    for g in range(GROUPS):
        at = pl.ds(g * group, group)
        copies.append(pltpu.make_async_copy(blocks_ref.at[at, pl.ds(first, count)], held_ref.at[at], sems.at[g]))
    for copy in copies:
        copy.start()
    return copies


def local_kernel(rows, size, last, x_ref, *refs):
    if last:
        blocks_ref, o_ref, held_ref, sems = refs
    else:
        w_ref, blocks_ref, o_ref, far_ref, held_ref, sems, far_sem = refs
    copies = fetch(blocks_ref, 0, held_ref, sems)
    if not last:
        later = pltpu.make_async_copy(blocks_ref.at[pl.ds(0, AHEAD), 3], far_ref, far_sem)
        later.start()
    for b in range(rows):
        if b % (rows // GROUPS) == 0:
            copies[b // (rows // GROUPS)].wait()
        acc = dot(x_ref[:, b * size:(b + 1) * size], held_ref[b, 0], NT)
        if b > 0:
            acc += dot(x_ref[:, (b - 1) * size:b * size], held_ref[b, 1], NT)
        if b < rows - 1:
            acc += dot(x_ref[:, (b + 1) * size:(b + 2) * size], held_ref[b, 2], NT)
        at = pl.ds(b * size, size)
        o_ref[:, at] = acc if last else w_ref[:, at] + STEP * acc
    if not last:
        later.wait()


def local_part(blocks, x, *w):
    width, states = x.shape
    rows, _, size, _ = blocks.shape
    out = [jax.ShapeDtypeStruct((width, states), F32)]
    scratch = [pltpu.VMEM((rows, 3, size, size), BF), pltpu.SemaphoreType.DMA((GROUPS,))]
    if w:
        out.append(pltpu.VMEM((AHEAD, size, size), BF))
        scratch.append(pltpu.SemaphoreType.DMA)
    return pl.pallas_call(
        functools.partial(local_kernel, rows, size, not w),
        out_shape=out,
        in_specs=[VMEM] * (1 + len(w)) + [HBM],
        out_specs=[VMEM] * len(out),
        scratch_shapes=scratch,
        compiler_params=pltpu.CompilerParams(vmem_limit_bytes=24 << 20),
        cost_estimate=pl.CostEstimate(
            flops=6 * width * rows * size * size, bytes_accessed=6 * rows * size * size, transcendentals=0
        ),
    )(x, *w, blocks)


def stream_far(blocks_ref, held_ref, edge_ref, sems):
    rows = blocks_ref.shape[0]
    ahead = rows - held_ref.shape[0]
    group = held_ref.shape[0] // LATER
    copies = []
    for g in range(LATER):
        source = blocks_ref.at[pl.ds(ahead + g * group, group), 3]
        copies.append(pltpu.make_async_copy(source, held_ref.at[pl.ds(g * group, group)], sems.at[g]))
    copies.append(pltpu.make_async_copy(blocks_ref.at[0, 1], edge_ref.at[0], sems.at[LATER]))
    copies.append(pltpu.make_async_copy(blocks_ref.at[rows - 1, 2], edge_ref.at[1], sems.at[LATER + 1]))
    for copy in copies:
        copy.start()
    waiting = set(range(LATER + 2))

    def wait(b):
        needed = []
        if b >= ahead:
            needed.append((b - ahead) // group)
        if b in (0, rows - 1):
            needed += [LATER, LATER + 1]
        for k in needed:
            if k in waiting:
                waiting.remove(k)
                copies[k].wait()
    return wait


def stream_scratch(held, size):
    return [
        pltpu.VMEM((held, size, size), BF),
        pltpu.VMEM((2, size, size), BF),
        pltpu.SemaphoreType.DMA((LATER + 2,)),
    ]


def far_sum(b, rows, odd_ref, loc_ref, recv_ref, pair_ref, other_ref, edge_ref, block):
    acc = dot(recv_ref[loc_ref[b]], block, NT)
    odd = odd_ref[0] == 1
    if b == 0:
        acc += dot(jnp.where(odd, pair_ref[...], other_ref[...]), edge_ref[0], NT)
    if b == rows - 1:
        acc += dot(jnp.where(odd, other_ref[...], pair_ref[...]), edge_ref[1], NT)
    return acc


def block_order(rows):
    return [*range(1, rows), 0]


def pack(want_ref, x_ref, send_ref, size):
    for s in range(send_ref.shape[0]):
        at = pl.multiple_of(want_ref[s] * size, size)
        send_ref[s] = x_ref[:, pl.ds(at, size)]


def far_kernel(rows, size, odd_ref, want_ref, loc_ref, t_ref, recv_ref, pair_ref, other_ref, far_ref, blocks_ref,
               w_ref, x_ref, send_ref, to_pair_ref, to_other_ref, held_ref, edge_ref, sems):
    wait = stream_far(blocks_ref, held_ref, edge_ref, sems)
    for b in block_order(rows):
        wait(b)
        block = far_ref[b] if b < AHEAD else held_ref[b - AHEAD]
        acc = far_sum(b, rows, odd_ref, loc_ref, recv_ref, pair_ref, other_ref, edge_ref, block)
        at = pl.ds(b * size, size)
        new = t_ref[:, at] + STEP * acc
        w_ref[:, at] = new
        x_ref[:, at] = new.astype(BF)
    last = (rows - 1) * size
    to_pair_ref[...] = x_ref[:, pl.ds(pl.multiple_of((1 - odd_ref[0]) * last, size), size)]
    to_other_ref[...] = x_ref[:, pl.ds(pl.multiple_of(odd_ref[0] * last, size), size)]
    pack(want_ref, x_ref, send_ref, size)


def far_part(odd, want, loc, t, recv, pair, other, far, blocks):
    width, states = t.shape
    size = far.shape[2]
    rows = states // size
    shapes = [
        jax.ShapeDtypeStruct((width, states), F32),
        jax.ShapeDtypeStruct((width, states), BF),
        jax.ShapeDtypeStruct(recv.shape, BF),
        jax.ShapeDtypeStruct((width, size), BF),
        jax.ShapeDtypeStruct((width, size), BF),
    ]
    return pl.pallas_call(
        functools.partial(far_kernel, rows, size),
        out_shape=shapes,
        in_specs=[SMEM] * 3 + [VMEM] * 5 + [HBM],
        out_specs=[VMEM] * len(shapes),
        scratch_shapes=stream_scratch(rows - AHEAD, size),
        compiler_params=pltpu.CompilerParams(vmem_limit_bytes=16 << 20),
        cost_estimate=pl.CostEstimate(
            flops=2 * width * rows * size * size, bytes_accessed=2 * rows * size * size, transcendentals=0
        ),
    )(odd, want, loc, t, recv, pair, other, far, blocks)


def applied_kernel(rows, size, odd_ref, loc_ref, t_ref, recv_ref, pair_ref, other_ref, blocks_ref, z_ref,
                   held_ref, edge_ref, sems):
    width = t_ref.shape[0]
    wait = stream_far(blocks_ref, held_ref, edge_ref, sems)
    for b in block_order(rows):
        wait(b)
        acc = far_sum(b, rows, odd_ref, loc_ref, recv_ref, pair_ref, other_ref, edge_ref, held_ref[b])
        at = pl.ds(b * size, size)
        z = t_ref[:, at] + acc
        top = z.astype(BF)
        z_ref[:width, at] = top
        z_ref[width:, at] = (z - top.astype(F32)).astype(BF)


def applied(odd, loc, t, recv, pair, other, blocks):
    width, states = t.shape
    size = blocks.shape[2]
    rows = states // size
    return pl.pallas_call(
        functools.partial(applied_kernel, rows, size),
        out_shape=jax.ShapeDtypeStruct((2 * width, states), BF),
        in_specs=[SMEM] * 2 + [VMEM] * 4 + [HBM],
        out_specs=VMEM,
        scratch_shapes=stream_scratch(rows, size),
        compiler_params=pltpu.CompilerParams(vmem_limit_bytes=16 << 20),
        cost_estimate=pl.CostEstimate(
            flops=2 * width * rows * size * size, bytes_accessed=2 * rows * size * size, transcendentals=0
        ),
    )(odd, loc, t, recv, pair, other, blocks)


def strips(all_ref, wide=2048):
    groups, width, states = all_ref.shape
    for start in range(0, states, wide):
        yield start, all_ref[:, :, start:start + wide].reshape(groups * width, wide)


def fold(a):
    half = a.shape[0] // 2
    return jnp.concatenate([a[:half], a[half:]], axis=1)


def unfold(a):
    half = a.shape[1] // 2
    return jnp.concatenate([a[:, :half], a[:, half:]], axis=0)


def sums_kernel(own_ref, z_ref, *refs):
    pieces, (o_ref, all_ref) = refs[:-2], refs[-2:]
    groups = len(pieces)
    width = z_ref.shape[0] // 2
    for k, piece in enumerate(pieces):
        all_ref[lax.rem(own_ref[0] + groups - k, groups)] = piece[...]
    total = jnp.zeros((3 * width, groups * width), F32)
    for start, w in strips(all_ref):
        at = pl.ds(start, w.shape[1])
        total += dot(jnp.concatenate([pieces[0][:, at], z_ref[:, at]], axis=0), w, NT)
    folded = jnp.concatenate([fold(total[:width]), fold(total[width:2 * width] + total[2 * width:])], axis=0)
    for c in range(o_ref.shape[0]):
        o_ref[c] = folded


def sums(own, z, pieces, copies):
    groups = len(pieces)
    width, states = pieces[0].shape
    modes = groups * width
    return pl.pallas_call(
        sums_kernel,
        out_shape=[
            jax.ShapeDtypeStruct((copies, width, 2 * modes), F32),
            jax.ShapeDtypeStruct((groups, width, states), BF),
        ],
        in_specs=[SMEM] + [VMEM] * (1 + groups),
        out_specs=[VMEM] * 2,
        compiler_params=pltpu.CompilerParams(vmem_limit_bytes=16 << 20),
        cost_estimate=pl.CostEstimate(
            flops=6 * width * modes * states, bytes_accessed=4 * modes * states, transcendentals=0
        ),
    )(own, z, *pieces)


def inverse_factor(gram):
    n = gram.shape[0]
    high = 8
    row_id = lax.broadcasted_iota(jnp.int32, (n, 2 * n), 0)
    lane = lax.broadcasted_iota(jnp.int32, (n, 2 * n), 1)
    unit = jnp.where(lane == row_id + n, 1.0, 0.0)
    work = jnp.concatenate([gram, unit[:, n:]], axis=1)
    slabs = [work[i:i + high] for i in range(0, n, high)]
    within = lax.broadcasted_iota(jnp.int32, (high, 1), 0)
    for j in range(0, n, 2):
        at, place = divmod(j, high)
        ones = [jnp.broadcast_to(slabs[i][:, j:j + 1], (high, 2 * n)) for i in range(at, n // high)]
        twos = [jnp.broadcast_to(slabs[i][:, j + 1:j + 2], (high, 2 * n)) for i in range(at, n // high)]
        first, second = slabs[at][place:place + 1], slabs[at][place + 1:place + 2]
        over = 1.0 / ones[0][place:place + 1]
        beside = ones[0][place + 1:place + 2]
        ratio = beside * over
        over_next = 1.0 / (twos[0][place + 1:place + 2] - beside * ratio)
        scaled = first * over
        scaled_next = (second - beside * scaled) * over_next
        for i in range(at, n // high):
            one, two = ones[i - at], twos[i - at] - ones[i - at] * ratio
            if i == at:
                one = jnp.where(within > place, one, 0.0)
                two = jnp.where(within > place + 1, two, 0.0)
            slabs[i] = slabs[i] - one * scaled - two * scaled_next
    work = jnp.concatenate(slabs, axis=0)
    pivots = jnp.sum(jnp.where(lane == row_id, work, 0.0), axis=1, keepdims=True)
    return work[:, n:] * lax.rsqrt(pivots)


def finish_kernel(scale, own_ref, parts_ref, all_ref, w_ref, out_ref, ritz_ref, inv_ref):
    groups, width, _ = all_ref.shape
    modes = groups * width
    half = width // 2
    gram, turned = [], []
    for c in range(groups):
        total = parts_ref[c]
        for r in range(1, parts_ref.shape[0] // groups):
            total = total + parts_ref[r * groups + c]
        gram.append(unfold(total[:half]))
        turned.append(unfold(total[half:]))
    inv_ref[...] = inverse_factor(jnp.concatenate(gram, axis=0) * scale)
    turned = jnp.concatenate(turned, axis=0) * scale
    start = pl.multiple_of(own_ref[0] * width, width)
    mine = inv_ref[pl.ds(start, width)]
    place = lax.broadcasted_iota(jnp.int32, (modes, width), 0) - lax.broadcasted_iota(jnp.int32, (modes, width), 1)
    pick = jnp.where(place == start, 1.0, 0.0)
    highest = lax.Precision.HIGHEST
    within = lax.dot_general(mine, pick, NN, precision=highest, preferred_element_type=F32)
    part = lax.dot_general(mine, turned, NN, precision=highest, preferred_element_type=F32)
    ritz_ref[...] = lax.dot_general(part, inv_ref[...], NT, precision=highest, preferred_element_type=F32)
    top = mine.astype(BF)
    rest = (mine - top.astype(F32)).astype(BF)
    left = jnp.concatenate([top, rest], axis=1)
    small = within.astype(BF)
    for first, w in strips(all_ref, 1024):
        at = pl.ds(first, w.shape[1])
        own = w_ref[:, at]
        low = (own - own.astype(BF).astype(F32)).astype(BF)
        acc = dot(left, jnp.concatenate([w, w], axis=0), NN)
        out_ref[:, at] = acc + dot(small, low, NN)


def finish(own, parts, everyone, w, scale):
    width, states = w.shape
    modes = everyone.shape[0] * width
    return pl.pallas_call(
        functools.partial(finish_kernel, scale),
        out_shape=[jax.ShapeDtypeStruct((width, states), F32), jax.ShapeDtypeStruct((width, modes), F32)],
        in_specs=[SMEM] + [VMEM] * 3,
        out_specs=[VMEM] * 2,
        scratch_shapes=[pltpu.VMEM((modes, modes), F32)],
        compiler_params=pltpu.CompilerParams(vmem_limit_bytes=16 << 20),
        cost_estimate=pl.CostEstimate(flops=1 << 30, bytes_accessed=16 << 20, transcendentals=0),
    )(own, parts, everyone, w)


def ask_kernel(rows, far_ref, o_ref):
    devices, lanes = o_ref.shape
    owner = lax.broadcasted_iota(jnp.int32, (devices, rows), 0)
    inside = jnp.broadcast_to(far_ref[...], (devices, rows)) - owner * rows
    match = jnp.logical_and(inside >= 0, inside < rows)
    first = jnp.min(jnp.where(match, inside, rows - 1), axis=1, keepdims=True)
    second = jnp.max(jnp.where(match, inside, 0), axis=1, keepdims=True)
    lane = lax.broadcasted_iota(jnp.int32, (devices, lanes), 1)
    o_ref[...] = jnp.where(lane == 0, first, second)


def first_pack_kernel(size, rows, answer_ref, x_ref, send_ref):
    for s in range(send_ref.shape[0]):
        block = jnp.clip(answer_ref[s // CAP, 0, s % CAP], 0, rows - 1)
        at = pl.multiple_of(block * size, size)
        send_ref[s] = x_ref[:, pl.ds(at, size)]


def body(basis, blocks, far_cols):
    width, states = basis.shape
    rows, _, size, _ = blocks.shape
    devices = lax.axis_size("rows")
    groups = lax.axis_size("cols")
    scale = 1.0 / (states * devices)
    both = ("rows", "cols")

    asked = pl.pallas_call(
        functools.partial(ask_kernel, rows),
        out_shape=jax.ShapeDtypeStruct((devices, 128), jnp.int32),
        in_specs=[VMEM],
        out_specs=VMEM,
        compiler_params=pltpu.CompilerParams(vmem_limit_bytes=1 << 20),
    )(far_cols.reshape(1, rows))
    answer = exchange(asked.reshape(devices, 1, 128), "rows")
    want = jnp.clip(answer[:, 0, :CAP].reshape(devices * CAP), 0, rows - 1)
    owner = far_cols // rows
    inside = far_cols % rows
    earlier = jnp.logical_and(owner[None, :] == owner[:, None], inside[None, :] < inside[:, None])
    loc = owner * CAP + jnp.any(earlier, axis=1).astype(jnp.int32)
    loc = jnp.clip(loc, 0, devices * CAP - 1)

    pairs = [(i, i + 1 - 2 * (i % 2)) for i in range(devices)]
    others = [(i, (i - 1 + 2 * (i % 2)) % devices) for i in range(devices)]
    odd = (lax.axis_index("rows") % 2).astype(jnp.int32)

    blocks = pltpu.with_memory_space_constraint(blocks, pltpu.HBM)
    w = basis
    x = w.astype(BF)
    send = pl.pallas_call(
        functools.partial(first_pack_kernel, size, rows),
        out_shape=jax.ShapeDtypeStruct((devices * CAP, width, size), BF),
        in_specs=[SMEM, VMEM],
        out_specs=VMEM,
        compiler_params=pltpu.CompilerParams(vmem_limit_bytes=2 << 20),
    )(answer, x)
    last = states - size
    to_pair = lax.dynamic_slice_in_dim(x, (1 - odd) * last, size, 1)
    to_other = lax.dynamic_slice_in_dim(x, odd * last, size, 1)
    odd = odd.reshape(1)
    for _ in range(ITERS):
        recv = exchange(send, "rows")
        pair = lax.ppermute(to_pair, "rows", pairs)
        other = lax.ppermute(to_other, "rows", others)
        t, far = local_part(blocks, x, w)
        w, x, send, to_pair, to_other = far_part(odd, want, loc, t, recv, pair, other, far, blocks)
    recv = exchange(send, "rows")
    pieces = [x]
    for k in range(1, groups):
        pieces.append(lax.ppermute(x, "cols", [(i, (i + k) % groups) for i in range(groups)]))
    pair = lax.ppermute(to_pair, "rows", pairs)
    other = lax.ppermute(to_other, "rows", others)
    t, = local_part(blocks, x)
    own = lax.axis_index("cols").reshape(1)
    z = applied(odd, loc, t, recv, pair, other, blocks)
    pieces, z = lax.optimization_barrier((pieces, z))
    parts, everyone = sums(own, z, pieces, devices * groups)
    basis_out, turned = finish(own, exchange(parts, both), everyone, w, scale)
    ritz = turned.T
    return (basis_out, ritz)


def solution(mesh):
    in_specs = (P("cols", "rows"), P("rows", None, None, None), P("rows"))
    out_specs = (P("cols", "rows"), P(None, "cols"))
    return jax.shard_map(body, mesh=mesh, in_specs=in_specs, out_specs=out_specs, check_vma=False)
```

```python
import functools

import jax
import jax.numpy as jnp
from jax import lax
from jax.experimental import pallas as pl
from jax.experimental.pallas import tpu as pltpu
from jax.sharding import PartitionSpec as P

ITERS = 4
CAP = 2
GROUPS = 4
AHEAD = 8
LATER = 2
PIVOTS = 8
STEP = 0.2
NT = (((1,), (1,)), ((), ()))
NN = (((1,), (0,)), ((), ()))
BF = jnp.bfloat16
F32 = jnp.float32
VMEM = pl.BlockSpec(memory_space=pltpu.VMEM)
SMEM = pl.BlockSpec(memory_space=pltpu.SMEM)
HBM = pl.BlockSpec(memory_space=pltpu.HBM)


def dot(a, b, dims):
    return lax.dot_general(a, b, dims, preferred_element_type=F32)


def exchange(x, axes):
    return lax.all_to_all(x, axes, split_axis=0, concat_axis=0, tiled=True)


def fetch(blocks_ref, first, held_ref, sems):
    rows, count = held_ref.shape[:2]
    group = rows // GROUPS
    copies = []
    for g in range(GROUPS):
        at = pl.ds(g * group, group)
        copies.append(pltpu.make_async_copy(blocks_ref.at[at, pl.ds(first, count)], held_ref.at[at], sems.at[g]))
    for copy in copies:
        copy.start()
    return copies


def local_kernel(rows, size, last, x_ref, *refs):
    if last:
        blocks_ref, o_ref, held_ref, sems = refs
    else:
        w_ref, blocks_ref, o_ref, far_ref, held_ref, sems, far_sem = refs
    copies = fetch(blocks_ref, 0, held_ref, sems)
    if not last:
        later = pltpu.make_async_copy(blocks_ref.at[pl.ds(0, AHEAD), 3], far_ref, far_sem)
        later.start()
    for b in range(rows):
        if b % (rows // GROUPS) == 0:
            copies[b // (rows // GROUPS)].wait()
        acc = dot(x_ref[:, b * size:(b + 1) * size], held_ref[b, 0], NT)
        if b > 0:
            acc += dot(x_ref[:, (b - 1) * size:b * size], held_ref[b, 1], NT)
        if b < rows - 1:
            acc += dot(x_ref[:, (b + 1) * size:(b + 2) * size], held_ref[b, 2], NT)
        at = pl.ds(b * size, size)
        o_ref[:, at] = acc if last else w_ref[:, at] + STEP * acc
    if not last:
        later.wait()


def local_part(blocks, x, *w):
    width, states = x.shape
    rows, _, size, _ = blocks.shape
    out = [jax.ShapeDtypeStruct((width, states), F32)]
    scratch = [pltpu.VMEM((rows, 3, size, size), BF), pltpu.SemaphoreType.DMA((GROUPS,))]
    if w:
        out.append(pltpu.VMEM((AHEAD, size, size), BF))
        scratch.append(pltpu.SemaphoreType.DMA)
    return pl.pallas_call(
        functools.partial(local_kernel, rows, size, not w),
        out_shape=out,
        in_specs=[VMEM] * (1 + len(w)) + [HBM],
        out_specs=[VMEM] * len(out),
        scratch_shapes=scratch,
        compiler_params=pltpu.CompilerParams(vmem_limit_bytes=24 << 20),
        cost_estimate=pl.CostEstimate(
            flops=6 * width * rows * size * size, bytes_accessed=6 * rows * size * size, transcendentals=0
        ),
    )(x, *w, blocks)


def stream_far(blocks_ref, held_ref, edge_ref, sems):
    rows = blocks_ref.shape[0]
    ahead = rows - held_ref.shape[0]
    group = held_ref.shape[0] // LATER
    copies = []
    for g in range(LATER):
        source = blocks_ref.at[pl.ds(ahead + g * group, group), 3]
        copies.append(pltpu.make_async_copy(source, held_ref.at[pl.ds(g * group, group)], sems.at[g]))
    copies.append(pltpu.make_async_copy(blocks_ref.at[0, 1], edge_ref.at[0], sems.at[LATER]))
    copies.append(pltpu.make_async_copy(blocks_ref.at[rows - 1, 2], edge_ref.at[1], sems.at[LATER + 1]))
    for copy in copies:
        copy.start()
    waiting = set(range(LATER + 2))

    def wait(b):
        needed = []
        if b >= ahead:
            needed.append((b - ahead) // group)
        if b in (0, rows - 1):
            needed += [LATER, LATER + 1]
        for k in needed:
            if k in waiting:
                waiting.remove(k)
                copies[k].wait()
    return wait


def stream_scratch(held, size):
    return [
        pltpu.VMEM((held, size, size), BF),
        pltpu.VMEM((2, size, size), BF),
        pltpu.SemaphoreType.DMA((LATER + 2,)),
    ]


def far_sum(b, rows, odd_ref, loc_ref, recv_ref, pair_ref, other_ref, edge_ref, block):
    acc = dot(recv_ref[loc_ref[b]], block, NT)
    odd = odd_ref[0] == 1
    if b == 0:
        acc += dot(jnp.where(odd, pair_ref[...], other_ref[...]), edge_ref[0], NT)
    if b == rows - 1:
        acc += dot(jnp.where(odd, other_ref[...], pair_ref[...]), edge_ref[1], NT)
    return acc


def block_order(rows):
    return [*range(1, rows), 0]


def pack(want_ref, x_ref, send_ref, size):
    for s in range(send_ref.shape[0]):
        at = pl.multiple_of(want_ref[s] * size, size)
        send_ref[s] = x_ref[:, pl.ds(at, size)]


def far_kernel(rows, size, last_one, odd_ref, want_ref, loc_ref, t_ref, recv_ref, pair_ref, other_ref, far_ref, blocks_ref,
               w_ref, x_ref, send_ref, to_pair_ref, to_other_ref, held_ref, edge_ref, sems):
    wait = stream_far(blocks_ref, held_ref, edge_ref, sems)
    for b in block_order(rows):
        wait(b)
        block = far_ref[b] if b < AHEAD else held_ref[b - AHEAD]
        acc = far_sum(b, rows, odd_ref, loc_ref, recv_ref, pair_ref, other_ref, edge_ref, block)
        at = pl.ds(b * size, size)
        new = t_ref[:, at] + STEP * acc
        rounded = new.astype(BF)
        x_ref[:, at] = rounded
        w_ref[:, at] = (new - rounded.astype(F32)).astype(BF) if last_one else new
    last = (rows - 1) * size
    to_pair_ref[...] = x_ref[:, pl.ds(pl.multiple_of((1 - odd_ref[0]) * last, size), size)]
    to_other_ref[...] = x_ref[:, pl.ds(pl.multiple_of(odd_ref[0] * last, size), size)]
    pack(want_ref, x_ref, send_ref, size)


def far_part(odd, want, loc, t, recv, pair, other, far, blocks, last_one):
    width, states = t.shape
    size = far.shape[2]
    rows = states // size
    shapes = [
        jax.ShapeDtypeStruct((width, states), BF if last_one else F32),
        jax.ShapeDtypeStruct((width, states), BF),
        jax.ShapeDtypeStruct(recv.shape, BF),
        jax.ShapeDtypeStruct((width, size), BF),
        jax.ShapeDtypeStruct((width, size), BF),
    ]
    return pl.pallas_call(
        functools.partial(far_kernel, rows, size, last_one),
        out_shape=shapes,
        in_specs=[SMEM] * 3 + [VMEM] * 5 + [HBM],
        out_specs=[VMEM] * len(shapes),
        scratch_shapes=stream_scratch(rows - AHEAD, size),
        compiler_params=pltpu.CompilerParams(vmem_limit_bytes=16 << 20),
        cost_estimate=pl.CostEstimate(
            flops=2 * width * rows * size * size, bytes_accessed=2 * rows * size * size, transcendentals=0
        ),
    )(odd, want, loc, t, recv, pair, other, far, blocks)


def applied_kernel(rows, size, odd_ref, loc_ref, t_ref, recv_ref, pair_ref, other_ref, blocks_ref, z_ref,
                   held_ref, edge_ref, sems):
    width = t_ref.shape[0]
    wait = stream_far(blocks_ref, held_ref, edge_ref, sems)
    for b in block_order(rows):
        wait(b)
        acc = far_sum(b, rows, odd_ref, loc_ref, recv_ref, pair_ref, other_ref, edge_ref, held_ref[b])
        at = pl.ds(b * size, size)
        z = t_ref[:, at] + acc
        top = z.astype(BF)
        z_ref[:width, at] = top
        z_ref[width:, at] = (z - top.astype(F32)).astype(BF)


def applied(odd, loc, t, recv, pair, other, blocks):
    width, states = t.shape
    size = blocks.shape[2]
    rows = states // size
    return pl.pallas_call(
        functools.partial(applied_kernel, rows, size),
        out_shape=jax.ShapeDtypeStruct((2 * width, states), BF),
        in_specs=[SMEM] * 2 + [VMEM] * 4 + [HBM],
        out_specs=VMEM,
        scratch_shapes=stream_scratch(rows, size),
        compiler_params=pltpu.CompilerParams(vmem_limit_bytes=16 << 20),
        cost_estimate=pl.CostEstimate(
            flops=2 * width * rows * size * size, bytes_accessed=2 * rows * size * size, transcendentals=0
        ),
    )(odd, loc, t, recv, pair, other, blocks)


def strips(all_ref, wide=2048):
    groups, width, states = all_ref.shape
    for start in range(0, states, wide):
        yield start, all_ref[:, :, start:start + wide].reshape(groups * width, wide)


def fold(a):
    half = a.shape[0] // 2
    return jnp.concatenate([a[:half], a[half:]], axis=1)


def unfold(a):
    half = a.shape[1] // 2
    return jnp.concatenate([a[:, :half], a[:, half:]], axis=0)


def sums_kernel(own_ref, z_ref, *refs):
    pieces, (o_ref, all_ref) = refs[:-2], refs[-2:]
    groups = len(pieces)
    width = z_ref.shape[0] // 2
    for k, piece in enumerate(pieces):
        all_ref[lax.rem(own_ref[0] + groups - k, groups)] = piece[...]
    total = jnp.zeros((3 * width, groups * width), F32)
    for start, w in strips(all_ref):
        at = pl.ds(start, w.shape[1])
        total += dot(jnp.concatenate([pieces[0][:, at], z_ref[:, at]], axis=0), w, NT)
    folded = jnp.concatenate([fold(total[:width]), fold(total[width:2 * width] + total[2 * width:])], axis=0)
    for c in range(o_ref.shape[0]):
        o_ref[c] = folded


def sums(own, z, pieces, copies):
    groups = len(pieces)
    width, states = pieces[0].shape
    modes = groups * width
    return pl.pallas_call(
        sums_kernel,
        out_shape=[
            jax.ShapeDtypeStruct((copies, width, 2 * modes), F32),
            jax.ShapeDtypeStruct((groups, width, states), BF),
        ],
        in_specs=[SMEM] + [VMEM] * (1 + groups),
        out_specs=[VMEM] * 2,
        compiler_params=pltpu.CompilerParams(vmem_limit_bytes=16 << 20),
        cost_estimate=pl.CostEstimate(
            flops=6 * width * modes * states, bytes_accessed=4 * modes * states, transcendentals=0
        ),
    )(own, z, *pieces)


def inverse_factor(gram):
    n = gram.shape[0]
    high = 8
    row_id = lax.broadcasted_iota(jnp.int32, (n, 2 * n), 0)
    lane = lax.broadcasted_iota(jnp.int32, (n, 2 * n), 1)
    unit = jnp.where(lane == row_id + n, 1.0, 0.0)
    work = jnp.concatenate([gram, unit[:, n:]], axis=1)
    slabs = [work[i:i + high] for i in range(0, n, high)]
    within = lax.broadcasted_iota(jnp.int32, (high, 1), 0)
    for j in range(0, n, PIVOTS):
        at, place = divmod(j, high)
        count = n // high - at
        columns = [
            [jnp.broadcast_to(slabs[at + i][:, j + m:j + m + 1], (high, 2 * n)) for i in range(count)]
            for m in range(PIVOTS)
        ]
        rows = [slabs[at][place + m:place + m + 1] for m in range(PIVOTS)]
        for m in range(PIVOTS):
            column = columns[m]
            over = 1.0 / column[0][place + m:place + m + 1]
            rows[m] = rows[m] * over
            for k in range(m + 1, PIVOTS):
                rows[k] = rows[k] - column[0][place + k:place + k + 1] * rows[m]
                ratio = columns[k][0][place + m:place + m + 1] * over
                columns[k] = [c - d * ratio for c, d in zip(columns[k], column)]
        for i in range(count):
            for m in range(PIVOTS):
                column = columns[m][i]
                if i == 0:
                    column = jnp.where(within > place + m, column, 0.0)
                slabs[at + i] = slabs[at + i] - column * rows[m]
    work = jnp.concatenate(slabs, axis=0)
    pivots = jnp.sum(jnp.where(lane == row_id, work, 0.0), axis=1, keepdims=True)
    return work[:, n:] * lax.rsqrt(pivots)


def finish_kernel(scale, own_ref, parts_ref, all_ref, low_ref, out_ref, ritz_ref, inv_ref):
    groups, width, _ = all_ref.shape
    modes = groups * width
    half = width // 2
    gram, turned = [], []
    for c in range(groups):
        total = parts_ref[c]
        for r in range(1, parts_ref.shape[0] // groups):
            total = total + parts_ref[r * groups + c]
        gram.append(unfold(total[:half]))
        turned.append(unfold(total[half:]))
    inv_ref[...] = inverse_factor(jnp.concatenate(gram, axis=0) * scale)
    turned = jnp.concatenate(turned, axis=0) * scale
    start = pl.multiple_of(own_ref[0] * width, width)
    mine = inv_ref[pl.ds(start, width)]
    place = lax.broadcasted_iota(jnp.int32, (modes, width), 0) - lax.broadcasted_iota(jnp.int32, (modes, width), 1)
    pick = jnp.where(place == start, 1.0, 0.0)
    highest = lax.Precision.HIGHEST
    within = lax.dot_general(mine, pick, NN, precision=highest, preferred_element_type=F32)
    part = lax.dot_general(mine, turned, NN, precision=highest, preferred_element_type=F32)
    ritz_ref[...] = lax.dot_general(part, inv_ref[...], NT, precision=highest, preferred_element_type=F32)
    top = mine.astype(BF)
    rest = (mine - top.astype(F32)).astype(BF)
    left = jnp.concatenate([top, rest], axis=1)
    small = within.astype(BF)
    for first, w in strips(all_ref, 1024):
        at = pl.ds(first, w.shape[1])
        acc = dot(left, jnp.concatenate([w, w], axis=0), NN)
        out_ref[:, at] = acc + dot(small, low_ref[:, at], NN)


def finish(own, parts, everyone, low, scale):
    width, states = low.shape
    modes = everyone.shape[0] * width
    return pl.pallas_call(
        functools.partial(finish_kernel, scale),
        out_shape=[jax.ShapeDtypeStruct((width, states), F32), jax.ShapeDtypeStruct((width, modes), F32)],
        in_specs=[SMEM] + [VMEM] * 3,
        out_specs=[VMEM] * 2,
        scratch_shapes=[pltpu.VMEM((modes, modes), F32)],
        compiler_params=pltpu.CompilerParams(vmem_limit_bytes=16 << 20),
        cost_estimate=pl.CostEstimate(flops=1 << 30, bytes_accessed=16 << 20, transcendentals=0),
    )(own, parts, everyone, low)


def ask_kernel(rows, far_ref, o_ref):
    devices, lanes = o_ref.shape
    owner = lax.broadcasted_iota(jnp.int32, (devices, rows), 0)
    inside = jnp.broadcast_to(far_ref[...], (devices, rows)) - owner * rows
    match = jnp.logical_and(inside >= 0, inside < rows)
    first = jnp.min(jnp.where(match, inside, rows - 1), axis=1, keepdims=True)
    second = jnp.max(jnp.where(match, inside, 0), axis=1, keepdims=True)
    lane = lax.broadcasted_iota(jnp.int32, (devices, lanes), 1)
    o_ref[...] = jnp.where(lane == 0, first, second)


def first_pack_kernel(size, rows, answer_ref, x_ref, send_ref):
    for s in range(send_ref.shape[0]):
        block = jnp.clip(answer_ref[s // CAP, 0, s % CAP], 0, rows - 1)
        at = pl.multiple_of(block * size, size)
        send_ref[s] = x_ref[:, pl.ds(at, size)]


def body(basis, blocks, far_cols):
    width, states = basis.shape
    rows, _, size, _ = blocks.shape
    devices = lax.axis_size("rows")
    groups = lax.axis_size("cols")
    scale = 1.0 / (states * devices)
    both = ("rows", "cols")

    asked = pl.pallas_call(
        functools.partial(ask_kernel, rows),
        out_shape=jax.ShapeDtypeStruct((devices, 128), jnp.int32),
        in_specs=[VMEM],
        out_specs=VMEM,
        compiler_params=pltpu.CompilerParams(vmem_limit_bytes=1 << 20),
    )(far_cols.reshape(1, rows))
    answer = exchange(asked.reshape(devices, 1, 128), "rows")
    want = jnp.clip(answer[:, 0, :CAP].reshape(devices * CAP), 0, rows - 1)
    owner = far_cols // rows
    inside = far_cols % rows
    earlier = jnp.logical_and(owner[None, :] == owner[:, None], inside[None, :] < inside[:, None])
    loc = owner * CAP + jnp.any(earlier, axis=1).astype(jnp.int32)
    loc = jnp.clip(loc, 0, devices * CAP - 1)

    pairs = [(i, i + 1 - 2 * (i % 2)) for i in range(devices)]
    others = [(i, (i - 1 + 2 * (i % 2)) % devices) for i in range(devices)]
    odd = (lax.axis_index("rows") % 2).astype(jnp.int32)

    blocks = pltpu.with_memory_space_constraint(blocks, pltpu.HBM)
    w = basis
    x = w.astype(BF)
    send = pl.pallas_call(
        functools.partial(first_pack_kernel, size, rows),
        out_shape=jax.ShapeDtypeStruct((devices * CAP, width, size), BF),
        in_specs=[SMEM, VMEM],
        out_specs=VMEM,
        compiler_params=pltpu.CompilerParams(vmem_limit_bytes=2 << 20),
    )(answer, x)
    last = states - size
    to_pair = lax.dynamic_slice_in_dim(x, (1 - odd) * last, size, 1)
    to_other = lax.dynamic_slice_in_dim(x, odd * last, size, 1)
    odd = odd.reshape(1)
    for step in range(ITERS):
        recv = exchange(send, "rows")
        pair = lax.ppermute(to_pair, "rows", pairs)
        other = lax.ppermute(to_other, "rows", others)
        t, far = local_part(blocks, x, w)
        w, x, send, to_pair, to_other = far_part(
            odd, want, loc, t, recv, pair, other, far, blocks, step == ITERS - 1
        )
    recv = exchange(send, "rows")
    pieces = [x]
    for k in range(1, groups):
        pieces.append(lax.ppermute(x, "cols", [(i, (i + k) % groups) for i in range(groups)]))
    pair = lax.ppermute(to_pair, "rows", pairs)
    other = lax.ppermute(to_other, "rows", others)
    t, = local_part(blocks, x)
    own = lax.axis_index("cols").reshape(1)
    z = applied(odd, loc, t, recv, pair, other, blocks)
    pieces, z = lax.optimization_barrier((pieces, z))
    parts, everyone = sums(own, z, pieces, devices * groups)
    basis_out, turned = finish(own, exchange(parts, both), everyone, w, scale)
    ritz = turned.T
    return (basis_out, ritz)


def solution(mesh):
    in_specs = (P("cols", "rows"), P("rows", None, None, None), P("rows"))
    out_specs = (P("cols", "rows"), P(None, "cols"))
    return jax.shard_map(body, mesh=mesh, in_specs=in_specs, out_specs=out_specs, check_vma=False)
```

```python
import functools

import jax
import jax.numpy as jnp
from jax import lax
from jax.experimental import pallas as pl
from jax.experimental.pallas import tpu as pltpu
from jax.sharding import PartitionSpec as P

ITERS = 4
CAP = 2
GROUPS = 4
AHEAD = 8
LATER = 2
PIVOTS = 8
STEP = 0.2
NT = (((1,), (1,)), ((), ()))
NN = (((1,), (0,)), ((), ()))
BF = jnp.bfloat16
F32 = jnp.float32
VMEM = pl.BlockSpec(memory_space=pltpu.VMEM)
SMEM = pl.BlockSpec(memory_space=pltpu.SMEM)
HBM = pl.BlockSpec(memory_space=pltpu.HBM)


def dot(a, b, dims):
    return lax.dot_general(a, b, dims, preferred_element_type=F32)


def exchange(x, axes):
    return lax.all_to_all(x, axes, split_axis=0, concat_axis=0, tiled=True)


def fetch(blocks_ref, first, held_ref, sems):
    rows, count = held_ref.shape[:2]
    group = rows // GROUPS
    copies = []
    for g in range(GROUPS):
        at = pl.ds(g * group, group)
        copies.append(pltpu.make_async_copy(blocks_ref.at[at, pl.ds(first, count)], held_ref.at[at], sems.at[g]))
    for copy in copies:
        copy.start()
    return copies


def local_kernel(rows, size, last, x_ref, *refs):
    if last:
        blocks_ref, o_ref, held_ref, sems = refs
    else:
        w_ref, blocks_ref, o_ref, far_ref, held_ref, sems, far_sem = refs
    copies = fetch(blocks_ref, 0, held_ref, sems)
    if not last:
        later = pltpu.make_async_copy(blocks_ref.at[pl.ds(0, AHEAD), 3], far_ref, far_sem)
        later.start()
    for b in range(rows):
        if b % (rows // GROUPS) == 0:
            copies[b // (rows // GROUPS)].wait()
        acc = dot(x_ref[:, b * size:(b + 1) * size], held_ref[b, 0], NT)
        if b > 0:
            acc += dot(x_ref[:, (b - 1) * size:b * size], held_ref[b, 1], NT)
        if b < rows - 1:
            acc += dot(x_ref[:, (b + 1) * size:(b + 2) * size], held_ref[b, 2], NT)
        at = pl.ds(b * size, size)
        o_ref[:, at] = acc if last else w_ref[:, at] + STEP * acc
    if not last:
        later.wait()


def local_part(blocks, x, *w):
    width, states = x.shape
    rows, _, size, _ = blocks.shape
    out = [jax.ShapeDtypeStruct((width, states), F32)]
    scratch = [pltpu.VMEM((rows, 3, size, size), BF), pltpu.SemaphoreType.DMA((GROUPS,))]
    if w:
        out.append(pltpu.VMEM((AHEAD, size, size), BF))
        scratch.append(pltpu.SemaphoreType.DMA)
    return pl.pallas_call(
        functools.partial(local_kernel, rows, size, not w),
        out_shape=out,
        in_specs=[VMEM] * (1 + len(w)) + [HBM],
        out_specs=[VMEM] * len(out),
        scratch_shapes=scratch,
        compiler_params=pltpu.CompilerParams(vmem_limit_bytes=24 << 20),
        cost_estimate=pl.CostEstimate(
            flops=6 * width * rows * size * size, bytes_accessed=6 * rows * size * size, transcendentals=0
        ),
    )(x, *w, blocks)


def stream_far(blocks_ref, held_ref, edge_ref, sems):
    rows = blocks_ref.shape[0]
    ahead = rows - held_ref.shape[0]
    group = held_ref.shape[0] // LATER
    copies = []
    for g in range(LATER):
        source = blocks_ref.at[pl.ds(ahead + g * group, group), 3]
        copies.append(pltpu.make_async_copy(source, held_ref.at[pl.ds(g * group, group)], sems.at[g]))
    copies.append(pltpu.make_async_copy(blocks_ref.at[0, 1], edge_ref.at[0], sems.at[LATER]))
    copies.append(pltpu.make_async_copy(blocks_ref.at[rows - 1, 2], edge_ref.at[1], sems.at[LATER + 1]))
    for copy in copies:
        copy.start()
    waiting = set(range(LATER + 2))

    def wait(b):
        needed = []
        if b >= ahead:
            needed.append((b - ahead) // group)
        if b in (0, rows - 1):
            needed += [LATER, LATER + 1]
        for k in needed:
            if k in waiting:
                waiting.remove(k)
                copies[k].wait()
    return wait


def stream_scratch(held, size):
    return [
        pltpu.VMEM((held, size, size), BF),
        pltpu.VMEM((2, size, size), BF),
        pltpu.SemaphoreType.DMA((LATER + 2,)),
    ]


def far_sum(b, rows, odd_ref, loc_ref, recv_ref, pair_ref, other_ref, edge_ref, block):
    acc = dot(recv_ref[loc_ref[b]], block, NT)
    odd = odd_ref[0] == 1
    if b == 0:
        acc += dot(jnp.where(odd, pair_ref[...], other_ref[...]), edge_ref[0], NT)
    if b == rows - 1:
        acc += dot(jnp.where(odd, other_ref[...], pair_ref[...]), edge_ref[1], NT)
    return acc


def block_order(rows):
    return [*range(1, rows), 0]


def pack(want_ref, x_ref, send_ref, size):
    for s in range(send_ref.shape[0]):
        at = pl.multiple_of(want_ref[s] * size, size)
        send_ref[s] = x_ref[:, pl.ds(at, size)]


def far_kernel(rows, size, last_one, odd_ref, want_ref, loc_ref, t_ref, recv_ref, pair_ref, other_ref, far_ref, blocks_ref,
               w_ref, x_ref, send_ref, to_pair_ref, to_other_ref, held_ref, edge_ref, sems):
    wait = stream_far(blocks_ref, held_ref, edge_ref, sems)
    for b in block_order(rows):
        wait(b)
        block = far_ref[b] if b < AHEAD else held_ref[b - AHEAD]
        acc = far_sum(b, rows, odd_ref, loc_ref, recv_ref, pair_ref, other_ref, edge_ref, block)
        at = pl.ds(b * size, size)
        new = t_ref[:, at] + STEP * acc
        rounded = new.astype(BF)
        x_ref[:, at] = rounded
        w_ref[:, at] = (new - rounded.astype(F32)).astype(BF) if last_one else new
    last = (rows - 1) * size
    to_pair_ref[...] = x_ref[:, pl.ds(pl.multiple_of((1 - odd_ref[0]) * last, size), size)]
    to_other_ref[...] = x_ref[:, pl.ds(pl.multiple_of(odd_ref[0] * last, size), size)]
    pack(want_ref, x_ref, send_ref, size)


def far_part(odd, want, loc, t, recv, pair, other, far, blocks, last_one):
    width, states = t.shape
    size = far.shape[2]
    rows = states // size
    shapes = [
        jax.ShapeDtypeStruct((width, states), BF if last_one else F32),
        jax.ShapeDtypeStruct((width, states), BF),
        jax.ShapeDtypeStruct(recv.shape, BF),
        jax.ShapeDtypeStruct((width, size), BF),
        jax.ShapeDtypeStruct((width, size), BF),
    ]
    return pl.pallas_call(
        functools.partial(far_kernel, rows, size, last_one),
        out_shape=shapes,
        in_specs=[SMEM] * 3 + [VMEM] * 5 + [HBM],
        out_specs=[VMEM] * len(shapes),
        scratch_shapes=stream_scratch(rows - AHEAD, size),
        compiler_params=pltpu.CompilerParams(vmem_limit_bytes=16 << 20),
        cost_estimate=pl.CostEstimate(
            flops=2 * width * rows * size * size, bytes_accessed=2 * rows * size * size, transcendentals=0
        ),
    )(odd, want, loc, t, recv, pair, other, far, blocks)


def applied_kernel(rows, size, odd_ref, loc_ref, t_ref, recv_ref, pair_ref, other_ref, blocks_ref, z_ref,
                   held_ref, edge_ref, sems):
    width = t_ref.shape[0]
    wait = stream_far(blocks_ref, held_ref, edge_ref, sems)
    for b in block_order(rows):
        wait(b)
        acc = far_sum(b, rows, odd_ref, loc_ref, recv_ref, pair_ref, other_ref, edge_ref, held_ref[b])
        at = pl.ds(b * size, size)
        z = t_ref[:, at] + acc
        top = z.astype(BF)
        z_ref[:width, at] = top
        z_ref[width:, at] = (z - top.astype(F32)).astype(BF)


def applied(odd, loc, t, recv, pair, other, blocks):
    width, states = t.shape
    size = blocks.shape[2]
    rows = states // size
    return pl.pallas_call(
        functools.partial(applied_kernel, rows, size),
        out_shape=jax.ShapeDtypeStruct((2 * width, states), BF),
        in_specs=[SMEM] * 2 + [VMEM] * 4 + [HBM],
        out_specs=VMEM,
        scratch_shapes=stream_scratch(rows, size),
        compiler_params=pltpu.CompilerParams(vmem_limit_bytes=16 << 20),
        cost_estimate=pl.CostEstimate(
            flops=2 * width * rows * size * size, bytes_accessed=2 * rows * size * size, transcendentals=0
        ),
    )(odd, loc, t, recv, pair, other, blocks)


def strips(all_ref, wide=2048):
    groups, width, states = all_ref.shape
    for start in range(0, states, wide):
        yield start, all_ref[:, :, start:start + wide].reshape(groups * width, wide)


def fold(a):
    half = a.shape[0] // 2
    return jnp.concatenate([a[:half], a[half:]], axis=1)


def unfold(a):
    half = a.shape[1] // 2
    return jnp.concatenate([a[:, :half], a[:, half:]], axis=0)


def sums_kernel(own_ref, z_ref, *refs):
    pieces, (o_ref, all_ref) = refs[:-2], refs[-2:]
    groups = len(pieces)
    width = z_ref.shape[0] // 2
    for k, piece in enumerate(pieces):
        all_ref[lax.rem(own_ref[0] + groups - k, groups)] = piece[...]
    total = jnp.zeros((3 * width, groups * width), F32)
    for start, w in strips(all_ref):
        at = pl.ds(start, w.shape[1])
        total += dot(jnp.concatenate([pieces[0][:, at], z_ref[:, at]], axis=0), w, NT)
    folded = jnp.concatenate([fold(total[:width]), fold(total[width:2 * width] + total[2 * width:])], axis=0)
    for c in range(o_ref.shape[0]):
        o_ref[c] = folded


def sums(own, z, pieces, copies):
    groups = len(pieces)
    width, states = pieces[0].shape
    modes = groups * width
    return pl.pallas_call(
        sums_kernel,
        out_shape=[
            jax.ShapeDtypeStruct((copies, width, 2 * modes), F32),
            jax.ShapeDtypeStruct((groups, width, states), BF),
        ],
        in_specs=[SMEM] + [VMEM] * (1 + groups),
        out_specs=[VMEM] * 2,
        compiler_params=pltpu.CompilerParams(vmem_limit_bytes=16 << 20),
        cost_estimate=pl.CostEstimate(
            flops=6 * width * modes * states, bytes_accessed=4 * modes * states, transcendentals=0
        ),
    )(own, z, *pieces)


def inverse_factor(gram):
    n = gram.shape[0]
    high = 8
    row_id = lax.broadcasted_iota(jnp.int32, (n, 2 * n), 0)
    lane = lax.broadcasted_iota(jnp.int32, (n, 2 * n), 1)
    unit = jnp.where(lane == row_id + n, 1.0, 0.0)
    work = jnp.concatenate([gram, unit[:, n:]], axis=1)
    slabs = [work[i:i + high] for i in range(0, n, high)]
    within = lax.broadcasted_iota(jnp.int32, (high, 1), 0)
    for j in range(0, n, PIVOTS):
        at, place = divmod(j, high)
        count = n // high - at
        columns = [
            [jnp.broadcast_to(slabs[at + i][:, j + m:j + m + 1], (high, 2 * n)) for i in range(count)]
            for m in range(PIVOTS)
        ]
        rows = [slabs[at][place + m:place + m + 1] for m in range(PIVOTS)]
        for m in range(PIVOTS):
            column = columns[m]
            over = 1.0 / column[0][place + m:place + m + 1]
            rows[m] = rows[m] * over
            for k in range(m + 1, PIVOTS):
                rows[k] = rows[k] - column[0][place + k:place + k + 1] * rows[m]
                ratio = columns[k][0][place + m:place + m + 1] * over
                columns[k] = [c - d * ratio for c, d in zip(columns[k], column)]
        for i in range(count):
            for m in range(PIVOTS):
                column = columns[m][i]
                if i == 0:
                    column = jnp.where(within > place + m, column, 0.0)
                slabs[at + i] = slabs[at + i] - column * rows[m]
    work = jnp.concatenate(slabs, axis=0)
    pivots = jnp.sum(jnp.where(lane == row_id, work, 0.0), axis=1, keepdims=True)
    return work[:, n:] * lax.rsqrt(pivots)


def finish_kernel(scale, own_ref, parts_ref, all_ref, low_ref, out_ref, ritz_ref, inv_ref):
    groups, width, _ = all_ref.shape
    modes = groups * width
    half = width // 2
    gram, turned = [], []
    for c in range(groups):
        total = parts_ref[c]
        for r in range(1, parts_ref.shape[0] // groups):
            total = total + parts_ref[r * groups + c]
        gram.append(unfold(total[:half]))
        turned.append(unfold(total[half:]))
    inv_ref[...] = inverse_factor(jnp.concatenate(gram, axis=0) * scale)
    turned = jnp.concatenate(turned, axis=0) * scale
    start = pl.multiple_of(own_ref[0] * width, width)
    mine = inv_ref[pl.ds(start, width)]
    place = lax.broadcasted_iota(jnp.int32, (modes, width), 0) - lax.broadcasted_iota(jnp.int32, (modes, width), 1)
    pick = jnp.where(place == start, 1.0, 0.0)
    highest = lax.Precision.HIGHEST
    within = lax.dot_general(mine, pick, NN, precision=highest, preferred_element_type=F32)
    part = lax.dot_general(mine, turned, NN, precision=highest, preferred_element_type=F32)
    ritz_ref[...] = lax.dot_general(part, inv_ref[...], NT, precision=highest, preferred_element_type=F32)
    top = mine.astype(BF)
    rest = (mine - top.astype(F32)).astype(BF)
    left = jnp.concatenate([top, rest], axis=1)
    small = within.astype(BF)
    for first, w in strips(all_ref, 1024):
        at = pl.ds(first, w.shape[1])
        acc = dot(left, jnp.concatenate([w, w], axis=0), NN)
        out_ref[:, at] = acc + dot(small, low_ref[:, at], NN)


def finish(own, parts, everyone, low, scale):
    width, states = low.shape
    modes = everyone.shape[0] * width
    return pl.pallas_call(
        functools.partial(finish_kernel, scale),
        out_shape=[jax.ShapeDtypeStruct((width, states), F32), jax.ShapeDtypeStruct((width, modes), F32)],
        in_specs=[SMEM] + [VMEM] * 3,
        out_specs=[VMEM] * 2,
        scratch_shapes=[pltpu.VMEM((modes, modes), F32)],
        compiler_params=pltpu.CompilerParams(vmem_limit_bytes=16 << 20),
        cost_estimate=pl.CostEstimate(flops=1 << 30, bytes_accessed=16 << 20, transcendentals=0),
    )(own, parts, everyone, low)


def ask_kernel(rows, far_ref, o_ref):
    devices, lanes = o_ref.shape
    owner = lax.broadcasted_iota(jnp.int32, (devices, rows), 0)
    inside = jnp.broadcast_to(far_ref[...], (devices, rows)) - owner * rows
    match = jnp.logical_and(inside >= 0, inside < rows)
    first = jnp.min(jnp.where(match, inside, rows - 1), axis=1, keepdims=True)
    second = jnp.max(jnp.where(match, inside, 0), axis=1, keepdims=True)
    lane = lax.broadcasted_iota(jnp.int32, (devices, lanes), 1)
    o_ref[...] = jnp.where(lane == 0, first, second)


def first_pack_kernel(size, want_ref, x_ref, send_ref):
    pack(want_ref, x_ref, send_ref, size)


def body(basis, blocks, far_cols):
    width, states = basis.shape
    rows, _, size, _ = blocks.shape
    devices = lax.axis_size("rows")
    groups = lax.axis_size("cols")
    scale = 1.0 / (states * devices)
    both = ("rows", "cols")

    asked = pl.pallas_call(
        functools.partial(ask_kernel, rows),
        out_shape=jax.ShapeDtypeStruct((devices, 128), jnp.int32),
        in_specs=[VMEM],
        out_specs=VMEM,
        compiler_params=pltpu.CompilerParams(vmem_limit_bytes=1 << 20),
    )(far_cols.reshape(1, rows))
    answer = exchange(asked.reshape(devices, 1, 128), "rows")
    want = jnp.clip(answer[:, 0, :CAP].reshape(devices * CAP), 0, rows - 1)
    owner = far_cols // rows
    inside = far_cols % rows
    earlier = jnp.logical_and(owner[None, :] == owner[:, None], inside[None, :] < inside[:, None])
    loc = owner * CAP + jnp.any(earlier, axis=1).astype(jnp.int32)
    loc = jnp.clip(loc, 0, devices * CAP - 1)

    pairs = [(i, i + 1 - 2 * (i % 2)) for i in range(devices)]
    others = [(i, (i - 1 + 2 * (i % 2)) % devices) for i in range(devices)]
    odd = (lax.axis_index("rows") % 2).astype(jnp.int32)

    blocks = pltpu.with_memory_space_constraint(blocks, pltpu.HBM)
    w = basis
    x = w.astype(BF)
    send = pl.pallas_call(
        functools.partial(first_pack_kernel, size),
        out_shape=jax.ShapeDtypeStruct((devices * CAP, width, size), BF),
        in_specs=[SMEM, VMEM],
        out_specs=VMEM,
        compiler_params=pltpu.CompilerParams(vmem_limit_bytes=2 << 20),
    )(want, x)
    last = states - size
    to_pair = lax.dynamic_slice_in_dim(x, (1 - odd) * last, size, 1)
    to_other = lax.dynamic_slice_in_dim(x, odd * last, size, 1)
    odd = odd.reshape(1)
    for step in range(ITERS):
        recv = exchange(send, "rows")
        pair = lax.ppermute(to_pair, "rows", pairs)
        other = lax.ppermute(to_other, "rows", others)
        t, far = local_part(blocks, x, w)
        w, x, send, to_pair, to_other = far_part(
            odd, want, loc, t, recv, pair, other, far, blocks, step == ITERS - 1
        )
    recv = exchange(send, "rows")
    pieces = [x]
    for k in range(1, groups):
        pieces.append(lax.ppermute(x, "cols", [(i, (i + k) % groups) for i in range(groups)]))
    pair = lax.ppermute(to_pair, "rows", pairs)
    other = lax.ppermute(to_other, "rows", others)
    t, = local_part(blocks, x)
    own = lax.axis_index("cols").reshape(1)
    z = applied(odd, loc, t, recv, pair, other, blocks)
    pieces, z = lax.optimization_barrier((pieces, z))
    parts, everyone = sums(own, z, pieces, devices * groups)
    basis_out, turned = finish(own, exchange(parts, both), everyone, w, scale)
    ritz = turned.T
    return (basis_out, ritz)


def solution(mesh):
    in_specs = (P("cols", "rows"), P("rows", None, None, None), P("rows"))
    out_specs = (P("cols", "rows"), P(None, "cols"))
    return jax.shard_map(body, mesh=mesh, in_specs=in_specs, out_specs=out_specs, check_vma=False)
```

```python
import functools

import jax
import jax.numpy as jnp
from jax import lax
from jax.experimental import pallas as pl
from jax.experimental.pallas import tpu as pltpu
from jax.sharding import PartitionSpec as P

ITERS = 4
CAP = 2
GROUPS = 8
AHEAD = 8
LATER = 2
PIVOTS = 8
STEP = 0.2
NT = (((1,), (1,)), ((), ()))
NN = (((1,), (0,)), ((), ()))
BF = jnp.bfloat16
F32 = jnp.float32
VMEM = pl.BlockSpec(memory_space=pltpu.VMEM)
SMEM = pl.BlockSpec(memory_space=pltpu.SMEM)
HBM = pl.BlockSpec(memory_space=pltpu.HBM)


def dot(a, b, dims):
    return lax.dot_general(a, b, dims, preferred_element_type=F32)


def exchange(x, axes):
    return lax.all_to_all(x, axes, split_axis=0, concat_axis=0, tiled=True)


def fetch(blocks_ref, first, held_ref, sems):
    rows, count = held_ref.shape[:2]
    group = rows // GROUPS
    copies = []
    for g in range(GROUPS):
        at = pl.ds(g * group, group)
        copies.append(pltpu.make_async_copy(blocks_ref.at[at, pl.ds(first, count)], held_ref.at[at], sems.at[g]))
    for copy in copies:
        copy.start()
    return copies


def local_kernel(rows, size, last, x_ref, *refs):
    if last:
        blocks_ref, o_ref, held_ref, sems = refs
    else:
        w_ref, blocks_ref, o_ref, far_ref, held_ref, sems, far_sem = refs
    copies = fetch(blocks_ref, 0, held_ref, sems)
    if not last:
        later = pltpu.make_async_copy(blocks_ref.at[pl.ds(0, AHEAD), 3], far_ref, far_sem)
        later.start()
    for b in range(rows):
        if b % (rows // GROUPS) == 0:
            copies[b // (rows // GROUPS)].wait()
        acc = dot(x_ref[:, b * size:(b + 1) * size], held_ref[b, 0], NT)
        if b > 0:
            acc += dot(x_ref[:, (b - 1) * size:b * size], held_ref[b, 1], NT)
        if b < rows - 1:
            acc += dot(x_ref[:, (b + 1) * size:(b + 2) * size], held_ref[b, 2], NT)
        at = pl.ds(b * size, size)
        o_ref[:, at] = acc if last else w_ref[:, at] + STEP * acc
    if not last:
        later.wait()


def local_part(blocks, x, *w):
    width, states = x.shape
    rows, _, size, _ = blocks.shape
    out = [jax.ShapeDtypeStruct((width, states), F32)]
    scratch = [pltpu.VMEM((rows, 3, size, size), BF), pltpu.SemaphoreType.DMA((GROUPS,))]
    if w:
        out.append(pltpu.VMEM((AHEAD, size, size), BF))
        scratch.append(pltpu.SemaphoreType.DMA)
    return pl.pallas_call(
        functools.partial(local_kernel, rows, size, not w),
        out_shape=out,
        in_specs=[VMEM] * (1 + len(w)) + [HBM],
        out_specs=[VMEM] * len(out),
        scratch_shapes=scratch,
        compiler_params=pltpu.CompilerParams(vmem_limit_bytes=24 << 20),
        cost_estimate=pl.CostEstimate(
            flops=6 * width * rows * size * size, bytes_accessed=6 * rows * size * size, transcendentals=0
        ),
    )(x, *w, blocks)


def stream_far(blocks_ref, held_ref, edge_ref, sems):
    rows = blocks_ref.shape[0]
    ahead = rows - held_ref.shape[0]
    group = held_ref.shape[0] // LATER
    copies = []
    for g in range(LATER):
        source = blocks_ref.at[pl.ds(ahead + g * group, group), 3]
        copies.append(pltpu.make_async_copy(source, held_ref.at[pl.ds(g * group, group)], sems.at[g]))
    copies.append(pltpu.make_async_copy(blocks_ref.at[0, 1], edge_ref.at[0], sems.at[LATER]))
    copies.append(pltpu.make_async_copy(blocks_ref.at[rows - 1, 2], edge_ref.at[1], sems.at[LATER + 1]))
    for copy in copies:
        copy.start()
    waiting = set(range(LATER + 2))

    def wait(b):
        needed = []
        if b >= ahead:
            needed.append((b - ahead) // group)
        if b in (0, rows - 1):
            needed += [LATER, LATER + 1]
        for k in needed:
            if k in waiting:
                waiting.remove(k)
                copies[k].wait()
    return wait


def stream_scratch(held, size):
    return [
        pltpu.VMEM((held, size, size), BF),
        pltpu.VMEM((2, size, size), BF),
        pltpu.SemaphoreType.DMA((LATER + 2,)),
    ]


def far_sum(b, rows, odd_ref, loc_ref, recv_ref, pair_ref, other_ref, edge_ref, block):
    acc = dot(recv_ref[loc_ref[b]], block, NT)
    odd = odd_ref[0] == 1
    if b == 0:
        acc += dot(jnp.where(odd, pair_ref[...], other_ref[...]), edge_ref[0], NT)
    if b == rows - 1:
        acc += dot(jnp.where(odd, other_ref[...], pair_ref[...]), edge_ref[1], NT)
    return acc


def block_order(rows):
    return [*range(1, rows), 0]


def pack(want_ref, x_ref, send_ref, size):
    for s in range(send_ref.shape[0]):
        at = pl.multiple_of(want_ref[s] * size, size)
        send_ref[s] = x_ref[:, pl.ds(at, size)]


def far_kernel(rows, size, last_one, odd_ref, want_ref, loc_ref, t_ref, recv_ref, pair_ref, other_ref, far_ref, blocks_ref,
               w_ref, x_ref, send_ref, to_pair_ref, to_other_ref, held_ref, edge_ref, sems):
    wait = stream_far(blocks_ref, held_ref, edge_ref, sems)
    for b in block_order(rows):
        wait(b)
        block = far_ref[b] if b < AHEAD else held_ref[b - AHEAD]
        acc = far_sum(b, rows, odd_ref, loc_ref, recv_ref, pair_ref, other_ref, edge_ref, block)
        at = pl.ds(b * size, size)
        new = t_ref[:, at] + STEP * acc
        rounded = new.astype(BF)
        x_ref[:, at] = rounded
        w_ref[:, at] = (new - rounded.astype(F32)).astype(BF) if last_one else new
    last = (rows - 1) * size
    to_pair_ref[...] = x_ref[:, pl.ds(pl.multiple_of((1 - odd_ref[0]) * last, size), size)]
    to_other_ref[...] = x_ref[:, pl.ds(pl.multiple_of(odd_ref[0] * last, size), size)]
    pack(want_ref, x_ref, send_ref, size)


def far_part(odd, want, loc, t, recv, pair, other, far, blocks, last_one):
    width, states = t.shape
    size = far.shape[2]
    rows = states // size
    shapes = [
        jax.ShapeDtypeStruct((width, states), BF if last_one else F32),
        jax.ShapeDtypeStruct((width, states), BF),
        jax.ShapeDtypeStruct(recv.shape, BF),
        jax.ShapeDtypeStruct((width, size), BF),
        jax.ShapeDtypeStruct((width, size), BF),
    ]
    return pl.pallas_call(
        functools.partial(far_kernel, rows, size, last_one),
        out_shape=shapes,
        in_specs=[SMEM] * 3 + [VMEM] * 5 + [HBM],
        out_specs=[VMEM] * len(shapes),
        scratch_shapes=stream_scratch(rows - AHEAD, size),
        compiler_params=pltpu.CompilerParams(vmem_limit_bytes=16 << 20),
        cost_estimate=pl.CostEstimate(
            flops=2 * width * rows * size * size, bytes_accessed=2 * rows * size * size, transcendentals=0
        ),
    )(odd, want, loc, t, recv, pair, other, far, blocks)


def applied_kernel(rows, size, odd_ref, loc_ref, t_ref, recv_ref, pair_ref, other_ref, blocks_ref, z_ref,
                   held_ref, edge_ref, sems):
    width = t_ref.shape[0]
    wait = stream_far(blocks_ref, held_ref, edge_ref, sems)
    for b in block_order(rows):
        wait(b)
        acc = far_sum(b, rows, odd_ref, loc_ref, recv_ref, pair_ref, other_ref, edge_ref, held_ref[b])
        at = pl.ds(b * size, size)
        z = t_ref[:, at] + acc
        top = z.astype(BF)
        z_ref[:width, at] = top
        z_ref[width:, at] = (z - top.astype(F32)).astype(BF)


def applied(odd, loc, t, recv, pair, other, blocks):
    width, states = t.shape
    size = blocks.shape[2]
    rows = states // size
    return pl.pallas_call(
        functools.partial(applied_kernel, rows, size),
        out_shape=jax.ShapeDtypeStruct((2 * width, states), BF),
        in_specs=[SMEM] * 2 + [VMEM] * 4 + [HBM],
        out_specs=VMEM,
        scratch_shapes=stream_scratch(rows, size),
        compiler_params=pltpu.CompilerParams(vmem_limit_bytes=16 << 20),
        cost_estimate=pl.CostEstimate(
            flops=2 * width * rows * size * size, bytes_accessed=2 * rows * size * size, transcendentals=0
        ),
    )(odd, loc, t, recv, pair, other, blocks)


def strips(all_ref, wide=2048):
    groups, width, states = all_ref.shape
    for start in range(0, states, wide):
        yield start, all_ref[:, :, start:start + wide].reshape(groups * width, wide)


def fold(a):
    half = a.shape[0] // 2
    return jnp.concatenate([a[:half], a[half:]], axis=1)


def unfold(a):
    half = a.shape[1] // 2
    return jnp.concatenate([a[:, :half], a[:, half:]], axis=0)


def sums_kernel(own_ref, z_ref, *refs):
    pieces, (o_ref, all_ref) = refs[:-2], refs[-2:]
    groups = len(pieces)
    width = z_ref.shape[0] // 2
    for k, piece in enumerate(pieces):
        all_ref[lax.rem(own_ref[0] + groups - k, groups)] = piece[...]
    total = jnp.zeros((3 * width, groups * width), F32)
    for start, w in strips(all_ref):
        at = pl.ds(start, w.shape[1])
        total += dot(jnp.concatenate([pieces[0][:, at], z_ref[:, at]], axis=0), w, NT)
    folded = jnp.concatenate([fold(total[:width]), fold(total[width:2 * width] + total[2 * width:])], axis=0)
    for c in range(o_ref.shape[0]):
        o_ref[c] = folded


def sums(own, z, pieces, copies):
    groups = len(pieces)
    width, states = pieces[0].shape
    modes = groups * width
    return pl.pallas_call(
        sums_kernel,
        out_shape=[
            jax.ShapeDtypeStruct((copies, width, 2 * modes), F32),
            jax.ShapeDtypeStruct((groups, width, states), BF),
        ],
        in_specs=[SMEM] + [VMEM] * (1 + groups),
        out_specs=[VMEM] * 2,
        compiler_params=pltpu.CompilerParams(vmem_limit_bytes=16 << 20),
        cost_estimate=pl.CostEstimate(
            flops=6 * width * modes * states, bytes_accessed=4 * modes * states, transcendentals=0
        ),
    )(own, z, *pieces)


def inverse_factor(gram):
    n = gram.shape[0]
    high = 8
    row_id = lax.broadcasted_iota(jnp.int32, (n, 2 * n), 0)
    lane = lax.broadcasted_iota(jnp.int32, (n, 2 * n), 1)
    unit = jnp.where(lane == row_id + n, 1.0, 0.0)
    work = jnp.concatenate([gram, unit[:, n:]], axis=1)
    slabs = [work[i:i + high] for i in range(0, n, high)]
    within = lax.broadcasted_iota(jnp.int32, (high, 1), 0)
    for j in range(0, n, PIVOTS):
        at, place = divmod(j, high)
        count = n // high - at
        columns = [
            [jnp.broadcast_to(slabs[at + i][:, j + m:j + m + 1], (high, 2 * n)) for i in range(count)]
            for m in range(PIVOTS)
        ]
        rows = [slabs[at][place + m:place + m + 1] for m in range(PIVOTS)]
        for m in range(PIVOTS):
            column = columns[m]
            over = 1.0 / column[0][place + m:place + m + 1]
            rows[m] = rows[m] * over
            for k in range(m + 1, PIVOTS):
                rows[k] = rows[k] - column[0][place + k:place + k + 1] * rows[m]
                ratio = columns[k][0][place + m:place + m + 1] * over
                columns[k] = [c - d * ratio for c, d in zip(columns[k], column)]
        for i in range(count):
            for m in range(PIVOTS):
                column = columns[m][i]
                if i == 0:
                    column = jnp.where(within > place + m, column, 0.0)
                slabs[at + i] = slabs[at + i] - column * rows[m]
    work = jnp.concatenate(slabs, axis=0)
    pivots = jnp.sum(jnp.where(lane == row_id, work, 0.0), axis=1, keepdims=True)
    return work[:, n:] * lax.rsqrt(pivots)


def finish_kernel(scale, own_ref, parts_ref, all_ref, low_ref, out_ref, ritz_ref, inv_ref):
    groups, width, _ = all_ref.shape
    modes = groups * width
    half = width // 2
    gram, turned = [], []
    for c in range(groups):
        total = parts_ref[c]
        for r in range(1, parts_ref.shape[0] // groups):
            total = total + parts_ref[r * groups + c]
        gram.append(unfold(total[:half]))
        turned.append(unfold(total[half:]))
    inv_ref[...] = inverse_factor(jnp.concatenate(gram, axis=0) * scale)
    turned = jnp.concatenate(turned, axis=0) * scale
    start = pl.multiple_of(own_ref[0] * width, width)
    mine = inv_ref[pl.ds(start, width)]
    place = lax.broadcasted_iota(jnp.int32, (modes, width), 0) - lax.broadcasted_iota(jnp.int32, (modes, width), 1)
    pick = jnp.where(place == start, 1.0, 0.0)
    highest = lax.Precision.HIGHEST
    within = lax.dot_general(mine, pick, NN, precision=highest, preferred_element_type=F32)
    part = lax.dot_general(mine, turned, NN, precision=highest, preferred_element_type=F32)
    ritz_ref[...] = lax.dot_general(part, inv_ref[...], NT, precision=highest, preferred_element_type=F32)
    top = mine.astype(BF)
    rest = (mine - top.astype(F32)).astype(BF)
    left = jnp.concatenate([top, rest], axis=1)
    small = within.astype(BF)
    for first, w in strips(all_ref, 1024):
        at = pl.ds(first, w.shape[1])
        acc = dot(left, jnp.concatenate([w, w], axis=0), NN)
        out_ref[:, at] = acc + dot(small, low_ref[:, at], NN)


def finish(own, parts, everyone, low, scale):
    width, states = low.shape
    modes = everyone.shape[0] * width
    return pl.pallas_call(
        functools.partial(finish_kernel, scale),
        out_shape=[jax.ShapeDtypeStruct((width, states), F32), jax.ShapeDtypeStruct((width, modes), F32)],
        in_specs=[SMEM] + [VMEM] * 3,
        out_specs=[VMEM] * 2,
        scratch_shapes=[pltpu.VMEM((modes, modes), F32)],
        compiler_params=pltpu.CompilerParams(vmem_limit_bytes=16 << 20),
        cost_estimate=pl.CostEstimate(flops=1 << 30, bytes_accessed=16 << 20, transcendentals=0),
    )(own, parts, everyone, low)


def ask_kernel(rows, far_ref, o_ref):
    devices, lanes = o_ref.shape
    owner = lax.broadcasted_iota(jnp.int32, (devices, rows), 0)
    inside = jnp.broadcast_to(far_ref[...], (devices, rows)) - owner * rows
    match = jnp.logical_and(inside >= 0, inside < rows)
    first = jnp.min(jnp.where(match, inside, rows - 1), axis=1, keepdims=True)
    second = jnp.max(jnp.where(match, inside, 0), axis=1, keepdims=True)
    lane = lax.broadcasted_iota(jnp.int32, (devices, lanes), 1)
    o_ref[...] = jnp.where(lane == 0, first, second)


def first_pack_kernel(size, want_ref, x_ref, send_ref):
    pack(want_ref, x_ref, send_ref, size)


def body(basis, blocks, far_cols):
    width, states = basis.shape
    rows, _, size, _ = blocks.shape
    devices = lax.axis_size("rows")
    groups = lax.axis_size("cols")
    scale = 1.0 / (states * devices)
    both = ("rows", "cols")

    asked = pl.pallas_call(
        functools.partial(ask_kernel, rows),
        out_shape=jax.ShapeDtypeStruct((devices, 128), jnp.int32),
        in_specs=[VMEM],
        out_specs=VMEM,
        compiler_params=pltpu.CompilerParams(vmem_limit_bytes=1 << 20),
    )(far_cols.reshape(1, rows))
    answer = exchange(asked.reshape(devices, 1, 128), "rows")
    want = jnp.clip(answer[:, 0, :CAP].reshape(devices * CAP), 0, rows - 1)
    owner = far_cols // rows
    inside = far_cols % rows
    earlier = jnp.logical_and(owner[None, :] == owner[:, None], inside[None, :] < inside[:, None])
    loc = owner * CAP + jnp.any(earlier, axis=1).astype(jnp.int32)
    loc = jnp.clip(loc, 0, devices * CAP - 1)

    pairs = [(i, i + 1 - 2 * (i % 2)) for i in range(devices)]
    others = [(i, (i - 1 + 2 * (i % 2)) % devices) for i in range(devices)]
    odd = (lax.axis_index("rows") % 2).astype(jnp.int32)

    blocks = pltpu.with_memory_space_constraint(blocks, pltpu.HBM)
    w = basis
    x = w.astype(BF)
    send = pl.pallas_call(
        functools.partial(first_pack_kernel, size),
        out_shape=jax.ShapeDtypeStruct((devices * CAP, width, size), BF),
        in_specs=[SMEM, VMEM],
        out_specs=VMEM,
        compiler_params=pltpu.CompilerParams(vmem_limit_bytes=2 << 20),
    )(want, x)
    last = states - size
    to_pair = lax.dynamic_slice_in_dim(x, (1 - odd) * last, size, 1)
    to_other = lax.dynamic_slice_in_dim(x, odd * last, size, 1)
    odd = odd.reshape(1)
    for step in range(ITERS):
        recv = exchange(send, "rows")
        pair = lax.ppermute(to_pair, "rows", pairs)
        other = lax.ppermute(to_other, "rows", others)
        t, far = local_part(blocks, x, w)
        w, x, send, to_pair, to_other = far_part(
            odd, want, loc, t, recv, pair, other, far, blocks, step == ITERS - 1
        )
    recv = exchange(send, "rows")
    pieces = [x]
    for k in range(1, groups):
        pieces.append(lax.ppermute(x, "cols", [(i, (i + k) % groups) for i in range(groups)]))
    pair = lax.ppermute(to_pair, "rows", pairs)
    other = lax.ppermute(to_other, "rows", others)
    t, = local_part(blocks, x)
    own = lax.axis_index("cols").reshape(1)
    z = applied(odd, loc, t, recv, pair, other, blocks)
    pieces, z = lax.optimization_barrier((pieces, z))
    parts, everyone = sums(own, z, pieces, devices * groups)
    basis_out, turned = finish(own, exchange(parts, both), everyone, w, scale)
    ritz = turned.T
    return (basis_out, ritz)


def solution(mesh):
    in_specs = (P("cols", "rows"), P("rows", None, None, None), P("rows"))
    out_specs = (P("cols", "rows"), P(None, "cols"))
    return jax.shard_map(body, mesh=mesh, in_specs=in_specs, out_specs=out_specs, check_vma=False)
```
